512 devices in a mesh: row: 32 (over y, x, z_hi), col: 16 (over z_lo, core).
Axes of the slice: x: 4, y: 4, z: 16 (z_hi: 2, z_lo: 8; z = z_hi * 8 + z_lo), core: 2. Of those that a mesh axis runs over, the one named last changes fastest.
Arguments:
- object_slices: float32 [2, 2, 4096, 2048], P(None, None, 'row', 'col'), may hold values from -4 to 4
- probe_wave: bfloat16 [2, 256, 256], replicated, may hold values from -4 to 4
- propagator_phase: bfloat16 [256, 256], replicated, may hold values from -3.140625 to 3.140625
- intensity: bfloat16 [32, 16, 2, 256, 256], P('row', 'col'), may hold values from 0.099609375 to 3
- centres: int32 [32, 16, 2, 2], P('row', 'col'), may hold values from 0 to 4095, as said below
- batch_order: int32 [32, 16, 2], P('row', 'col'), may hold values from -1 to 510, as said below
Outputs:
- object_gradient: float32 [2, 2, 4096, 2048], P(None, None, 'row', 'col')
- probe_gradient: float32 [2, 256, 256], P(None, 'row', 'col')
The draws below stay inside these ranges and needn't reach their ends.
Inputs may be any that keep to these rules, and one draw needn't show every extreme that they name: `centres`: slot c of tile (g, h) holds (row, column) pixel coordinates in the whole object that lie in that tile: rows g * 128 to (g + 1) * 128 - 1, columns h * 128 to (h + 1) * 128 - 1; empty slots hold a point of their tile too. `batch_order`: -1 marks an empty slot; the live slots of a tile come first and are numbered 0, 1, 2, ... in batch order, tile after tile in row-major order of tiles; some tile has all 2 slots live and some tile has none.
All inputs are finite; a program needn't handle non-finite values.
Results may differ from the reference program's by a relative error of at most 0.0003.
Values sent between devices are 32-bit elements; how exact they have to be, the bound alone decides.
No kernel may reach another device: no remote copies, remote signals or barrier semaphores. Data moves between devices by JAX's collectives and lax.ppermute only.
A program may use at most 64 MiB of HBM per device.

```python
import math
import jax
import jax.numpy as jnp
from jax import lax

WIN = 256
SLICES = 2
TILE_R = 128
TILE_C = 128
SLOTS = 2
GRID_R = 32
GRID_C = 16
OBJ_R = 4096
OBJ_C = 2048


def draw_centres(key, part):
    key = jax.random.fold_in(key, 23)
    row_key, col_key = jax.random.split(key)
    tile_top = (jnp.arange(GRID_R, dtype=jnp.int32) * TILE_R)[:, None, None]
    tile_left = (jnp.arange(GRID_C, dtype=jnp.int32) * TILE_C)[None, :, None]
    row_values = jax.random.randint(row_key, (GRID_R, GRID_C, SLOTS), 0, TILE_R) + tile_top
    col_values = jax.random.randint(col_key, (GRID_R, GRID_C, SLOTS), 0, TILE_C) + tile_left
    row_values = row_values.at[0, 0, 0].set(0).at[GRID_R - 1, GRID_C - 1, 0].set(OBJ_R - 1)
    col_values = col_values.at[0, 0, 0].set(0).at[GRID_R - 1, GRID_C - 1, 0].set(OBJ_C - 1)
    return jnp.stack([row_values, col_values], axis=-1).astype(jnp.int32)


def draw_batch_order(key, part):
    key = jax.random.fold_in(key, 41)
    tiles = GRID_R * GRID_C
    base_counts = jnp.arange(tiles, dtype=jnp.int32) % (SLOTS + 1)
    counts = jax.random.permutation(key, base_counts)
    slot_index = jnp.arange(SLOTS, dtype=jnp.int32)
    filled = (slot_index[None, :] < counts[:, None]).reshape(-1).astype(jnp.int32)
    ranked = jnp.cumsum(filled) - 1
    ordered = jnp.where(filled > 0, ranked, -1)
    return ordered.reshape(GRID_R, GRID_C, SLOTS).astype(jnp.int32)


def levels(key, shape, cuts, least, high):
    gain = 1.0
    for axis_at, blocks in cuts:
        steps = jax.random.uniform(jax.random.fold_in(jax.random.fold_in(key, 6), axis_at), (blocks,), jnp.float32, least / len(cuts), high / len(cuts))
        gain = gain * jnp.repeat(jnp.exp(steps), shape[axis_at] // blocks).reshape((-1,) + (1,) * (len(shape) - 1 - axis_at))
    return gain


def bell_draw(own_key, extent, spread, most, cuts=(), kind=jnp.bfloat16):
    values = jax.random.normal(own_key, extent, jnp.float32) * spread
    if len(cuts) > 0:
        values = levels(own_key, extent, cuts, -0.22, 0.18) * values
    return jnp.clip(values, min=-most, max=most).astype(kind)


def setup_inputs(seed: int = 0) -> dict:
    arg_keys = jax.random.split(jax.random.key(seed), 7)
    object_slices = bell_draw(arg_keys[0], (SLICES, 2, OBJ_R, OBJ_C), 0.7, 4.0, ((2, 32), (3, 16)), jnp.float32)
    probe_wave = bell_draw(arg_keys[1], (2, WIN, WIN), 0.7, 4.0)
    propagator_phase = jnp.clip(jax.random.uniform(arg_keys[2], (WIN, WIN), jnp.float32, -3.140625, 3.140625), -3.140625, 3.140625).astype(jnp.bfloat16)
    intensity = jnp.clip(jnp.exp(math.log(3.0) - 3.4051113 * jax.random.uniform(arg_keys[3], (GRID_R, GRID_C, SLOTS, WIN, WIN), jnp.float32) ** levels(arg_keys[3], (GRID_R, GRID_C, SLOTS, WIN, WIN), ((0, 32), (1, 16)), -0.2, 0.2)), 0.099609375, 3.0).astype(jnp.bfloat16)
    centres = draw_centres(jax.random.fold_in(arg_keys[6], 71), 0)
    batch_order = draw_batch_order(jax.random.fold_in(arg_keys[6], 71), 0)
    return dict(object_slices=object_slices, probe_wave=probe_wave, propagator_phase=propagator_phase, intensity=intensity, centres=centres, batch_order=batch_order)


def complex_pair(values):
    return jnp.stack([jnp.real(values), jnp.imag(values)])


def position_terms(padded, probe_field, propagator, row_start, col_start, measured, weight):
    zero_index = jnp.zeros((), jnp.int32)
    anchor = (zero_index, zero_index, row_start.astype(jnp.int32), col_start.astype(jnp.int32))
    window = lax.dynamic_slice(padded, anchor, (SLICES, 2, WIN, WIN))
    layers = lax.complex(window[:, 0], window[:, 1])
    wave_field = probe_field
    entering = []
    for slice_index in range(SLICES):
        entering.append(wave_field)
        spectrum = jnp.fft.fft2(wave_field * layers[slice_index], norm="ortho")
        if slice_index + 1 < SLICES:
            wave_field = jnp.fft.ifft2(spectrum * propagator, norm="ortho")
    power_map = jnp.real(spectrum) ** 2 + jnp.imag(spectrum) ** 2
    misfit = weight * (power_map - measured)
    adjoint = jnp.fft.ifft2(misfit * spectrum, norm="ortho")
    object_terms = [None] * SLICES
    for slice_index in reversed(range(SLICES)):
        object_terms[slice_index] = complex_pair(jnp.conj(entering[slice_index]) * adjoint)
        upstream = jnp.conj(layers[slice_index]) * adjoint
        if slice_index > 0:
            adjoint = jnp.fft.ifft2(jnp.fft.fft2(upstream, norm="ortho") * jnp.conj(propagator), norm="ortho")
    return jnp.stack(object_terms), complex_pair(upstream)


def reference(object_slices, probe_wave, propagator_phase, intensity, centres, batch_order):
    half_win = WIN // 2
    padded = jnp.pad(object_slices, ((0, 0), (0, 0), (half_win, half_win), (half_win, half_win)))
    probe_field = lax.complex(probe_wave[0].astype(jnp.float32), probe_wave[1].astype(jnp.float32))
    angles = propagator_phase.astype(jnp.float32)
    propagator = lax.complex(jnp.cos(angles), jnp.sin(angles))
    centre_list = centres.reshape(-1, 2).astype(jnp.int32)
    weights = (batch_order.reshape(-1) >= 0).astype(jnp.float32)
    measured = intensity.reshape(-1, WIN, WIN)

    def advance(state_pair, inputs):
        gradient, probe_sum = state_pair
        centre_pair, weight, frame_data = inputs
        window_terms, upstream = position_terms(padded, probe_field, propagator, centre_pair[0], centre_pair[1], frame_data.astype(jnp.float32), weight)
        zero_index = jnp.zeros((), jnp.int32)
        anchor = (zero_index, zero_index, centre_pair[0].astype(jnp.int32), centre_pair[1].astype(jnp.int32))
        current = lax.dynamic_slice(gradient, anchor, window_terms.shape)
        gradient = lax.dynamic_update_slice(gradient, current + window_terms, anchor)
        return (gradient, probe_sum + upstream), None

    initial = (jnp.zeros(padded.shape, jnp.float32), jnp.zeros((2, WIN, WIN), jnp.float32))
    (gradient, probe_sum), unused = lax.scan(advance, initial, (centre_list, weights, measured))
    return gradient[:, :, half_win:half_win + OBJ_R, half_win:half_win + OBJ_C], probe_sum
```

```python
import math

import jax
import jax.numpy as jnp
import numpy as np
from jax import lax
from jax.experimental import pallas as pl
from jax.experimental.pallas import tpu as pltpu
from jax.sharding import PartitionSpec as P

WIN = 256
HALF = 128
F32 = jnp.float32
BF16 = jnp.bfloat16


def frequency_order():
    return np.concatenate([np.arange(0, WIN, 2), np.arange(1, WIN, 2)])


def order_matrix():
    matrix = np.zeros((WIN, WIN), np.float32)
    matrix[np.arange(WIN), frequency_order()] = 1.0
    return jnp.asarray(matrix, BF16)


def half_tables():
    spots = np.arange(HALF)
    tables = []
    for parity in range(2):
        angles = 2.0 * math.pi * (np.outer(spots, 2 * spots + parity) % WIN) / WIN
        cosine, sine = (np.cos(angles) / 16.0, np.sin(angles) / 16.0)
        block = np.block([[cosine, -sine], [sine, cosine]])
        tables += [block, block.T]
    exact = np.stack(tables).astype(np.float32)
    high = exact.astype(jnp.bfloat16)
    low = (exact - high.astype(np.float32)).astype(jnp.bfloat16)
    return jnp.asarray(np.stack([high, low], axis=1))


def split(value):
    high = value.astype(BF16)
    return high, (value - high.astype(F32)).astype(BF16)


def dot(left, right):
    return jnp.dot(left, right, preferred_element_type=F32)


def right_mul(value, table_ref, index):
    high, low = split(value)
    table = table_ref[index, 0]
    return dot(high, table) + (dot(low, table) + dot(high, table_ref[index, 1]))


def left_mul(table_ref, index, value):
    high, low = split(value)
    table = table_ref[index, 0]
    return dot(table, high) + (dot(table, low) + dot(table_ref[index, 1], high))


def join(first, second, axis):
    return jnp.concatenate([first, second], axis=axis)


def halves(value, axis):
    if axis == 0:
        return value[:HALF], value[HALF:]
    return value[:, :HALF], value[:, HALF:]


def forward_axis(field, tables, axis):
    (re0, re1), (im0, im1) = (halves(field[0], axis), halves(field[1], axis))
    even = join(re0 + re1, im0 + im1, axis)
    odd = join(re0 - re1, im0 - im1, axis)
    if axis == 1:
        even, odd = (right_mul(even, tables, 0), right_mul(odd, tables, 2))
    else:
        even, odd = (left_mul(tables, 1, even), left_mul(tables, 3, odd))
    (re0, im0), (re1, im1) = (halves(even, axis), halves(odd, axis))
    return (join(re0, re1, axis), join(im0, im1, axis))


def inverse_axis(field, tables, axis):
    (re0, re1), (im0, im1) = (halves(field[0], axis), halves(field[1], axis))
    even = join(re0, im0, axis)
    odd = join(re1, im1, axis)
    if axis == 1:
        even, odd = (right_mul(even, tables, 1), right_mul(odd, tables, 3))
    else:
        even, odd = (left_mul(tables, 0, even), left_mul(tables, 2, odd))
    (re0, im0), (re1, im1) = (halves(even, axis), halves(odd, axis))
    return (join(re0 + re1, re0 - re1, axis), join(im0 + im1, im0 - im1, axis))


def forward(field, tables):
    return forward_axis(forward_axis(field, tables, 1), tables, 0)


def inverse(field, tables):
    return inverse_axis(inverse_axis(field, tables, 0), tables, 1)


def times(left, right):
    return (left[0] * right[0] - left[1] * right[1], left[0] * right[1] + left[1] * right[0])


def conj_times(left, right):
    return (left[0] * right[0] + left[1] * right[1], left[0] * right[1] - left[1] * right[0])


def cut_lanes(strip, shift):
    turned = [pltpu.roll(strip[:, k * HALF:(k + 1) * HALF], (HALF - shift) & (HALF - 1), 1) for k in range(3)]
    kept = lax.broadcasted_iota(jnp.int32, turned[0].shape, 1) < HALF - shift
    return jnp.concatenate([jnp.where(kept, turned[k], turned[k + 1]) for k in range(2)], axis=1)


def put_lanes(value, shift):
    turned = [pltpu.roll(value[:, k * HALF:(k + 1) * HALF], shift, 1) for k in range(2)]
    kept = lax.broadcasted_iota(jnp.int32, turned[0].shape, 1) >= shift
    return jnp.concatenate(
        [jnp.where(kept, turned[0], 0.0), jnp.where(kept, turned[1], turned[0]), jnp.where(kept, 0.0, turned[1])],
        axis=1,
    )


def cut_rows(strip, shift):
    groups = pltpu.roll(strip.reshape(WIN // 8 + 1, 8, strip.shape[1]), (8 - shift) & 7, 1)
    kept = lax.broadcasted_iota(jnp.int32, (WIN // 8, 8, strip.shape[1]), 1) < 8 - shift
    return jnp.where(kept, groups[:-1], groups[1:]).reshape(WIN, strip.shape[1])


def put_rows(value, shift):
    groups = pltpu.roll(value.reshape(WIN // 8, 8, value.shape[1]), shift, 1)
    none = jnp.zeros((1, 8, value.shape[1]), F32)
    kept = lax.broadcasted_iota(jnp.int32, (WIN // 8 + 1, 8, value.shape[1]), 1) >= shift
    here = jnp.concatenate([groups, none], axis=0)
    before = jnp.concatenate([none, groups], axis=0)
    return jnp.where(kept, here, before).reshape(WIN + 8, value.shape[1])


def work_kernel(place, weight, own, own_l, own_r, near, near_l, near_r, far, far_l, far_r,
                probe, propagator, intensity, tables, out_own, out_own_l, out_own_r, out_near,
                out_near_l, out_near_r, out_far, out_far_l, out_far_r, out_probe, extended, total):
    near_top = pl.multiple_of(place[4], HALF)
    far_top = pl.multiple_of(place[5], HALF)
    groups_in = ((far_top, (far_l, far, far_r)), (near_top, (near_l, near, near_r)), (HALF, (own_l, own, own_r)))
    for top, trio in groups_in:
        for k in range(3):
            for layer in range(2):
                for part in range(2):
                    extended[2 * layer + part, pl.ds(top, HALF), k * HALF:(k + 1) * HALF] = trio[k][layer, part]
    total[...] = jnp.zeros(total.shape, F32)
    wave = (probe[0].astype(F32), probe[1].astype(F32))
    spread = (propagator[0], propagator[1])
    for slot in range(2):
        row, col = (place[2 * slot], place[2 * slot + 1])

        low = row % 8
        base = pl.multiple_of(row - low, 8)

        def window(index):
            strip = extended[index, pl.ds(base, WIN + 8), :]
            return cut_rows(cut_lanes(strip, col), low)

        layer0 = (window(0), window(1))
        spectrum = forward(times(wave, layer0), tables)
        entering = inverse(times(spectrum, spread), tables)
        layer1 = (window(2), window(3))
        spectrum = forward(times(entering, layer1), tables)
        power = spectrum[0] * spectrum[0] + spectrum[1] * spectrum[1]
        misfit = weight[slot] * (power - intensity[slot])
        adjoint = inverse((misfit * spectrum[0], misfit * spectrum[1]), tables)
        term1 = conj_times(entering, adjoint)
        spectrum = forward(conj_times(layer1, adjoint), tables)
        adjoint = inverse(conj_times(spread, spectrum), tables)
        term0 = conj_times(wave, adjoint)
        upstream = conj_times(layer0, adjoint)
        for part in range(2):
            if slot == 0:
                out_probe[part] = upstream[part]
            else:
                out_probe[part] += upstream[part]

        def add_window(index, value):
            total[index, pl.ds(base, WIN + 8), :] += put_lanes(put_rows(value, low), col)

        for layer, term in ((0, term0), (1, term1)):
            for part in range(2):
                add_window(2 * layer + part, term[part])
    groups_out = ((far_top, (out_far_l, out_far, out_far_r)), (near_top, (out_near_l, out_near, out_near_r)), (HALF, (out_own_l, out_own, out_own_r)))
    for top, trio in groups_out:
        for k in range(3):
            for layer in range(2):
                for part in range(2):
                    trio[k][layer, part] = total[2 * layer + part, pl.ds(top, HALF), k * HALF:(k + 1) * HALF]


def work(place, weight, tiles, probe, propagator, intensity, tables):
    vmem = pl.BlockSpec(memory_space=pltpu.VMEM)
    smem = pl.BlockSpec(memory_space=pltpu.SMEM)
    tile = jax.ShapeDtypeStruct((2, 2, HALF, HALF), F32)
    return pl.pallas_call(
        work_kernel,
        out_shape=[tile] * 9 + [jax.ShapeDtypeStruct((2, WIN, WIN), F32)],
        in_specs=[smem, smem] + [vmem] * 13,
        out_specs=[vmem] * 10,
        scratch_shapes=[pltpu.VMEM((4, 3 * HALF, 3 * HALF), F32)] * 2,
        compiler_params=pltpu.CompilerParams(vmem_limit_bytes=48 * 1024 * 1024),
        cost_estimate=pl.CostEstimate(flops=10_000_000_000, bytes_accessed=8_000_000, transcendentals=0),
    )(place, weight, *tiles, probe, propagator, intensity, tables)


def pairs_up(count):
    return [(i, i + 1) for i in range(count - 1)]


def flipped(pairs):
    return [(j, i) for i, j in pairs]


def sides(value):
    ups = pairs_up(lax.axis_size("col"))
    return lax.ppermute(value, "col", ups), lax.ppermute(value, "col", flipped(ups))


def across(axis, bit):
    return [(i, i ^ bit) for i in range(lax.axis_size(axis))]


def probe_block(term):
    row, col = (lax.axis_index("row"), lax.axis_index("col"))
    rows, cols = (lax.axis_size("row"), lax.axis_size("col"))
    bit = rows // 2
    while bit >= 1:
        size = term.shape[1] // 2
        upper = (row // bit) % 2
        first, second = (term[:, :size], term[:, size:])
        kept = jnp.where(upper == 1, second, first)
        sent = jnp.where(upper == 1, first, second)
        term = kept + lax.ppermute(sent, "row", across("row", bit))
        bit //= 2
    bit = 1
    while bit < cols:
        term = term + lax.ppermute(term, "col", across("col", bit))
        bit *= 2
    width = WIN // cols
    return lax.dynamic_slice(term, (0, 0, col * width), (2, term.shape[1], width))


def per_device(object_slices, probe_wave, propagator_phase, intensity, centres, batch_order):
    rows = lax.axis_size("row")
    row, col = (lax.axis_index("row"), lax.axis_index("col"))
    hops = [(i, i + 2) for i in range(0, rows - 2, 2)] + [(i + 2, i) for i in range(1, rows - 2, 2)]
    swap = across("row", 1)
    near = lax.ppermute(object_slices, "row", swap)
    own_l, own_r = sides(object_slices)
    far = lax.ppermute(near, "row", hops)
    near_l, near_r = sides(near)
    far_l, far_r = sides(far)
    tiles = (object_slices, own_l, own_r, near, near_l, near_r, far, far_l, far_r)

    order = order_matrix()
    angles = dot(dot(order, propagator_phase).astype(BF16), order.T)
    propagator = jnp.stack([jnp.cos(angles), jnp.sin(angles)])
    middle = jnp.einsum("ab,sbc->sac", order, intensity[0, 0], preferred_element_type=F32).astype(BF16)
    measured = jnp.einsum("sac,dc->sad", middle, order, preferred_element_type=F32)
    upper = row % 2
    place = jnp.concatenate([
        (centres[0, 0] - jnp.stack([row * HALF, col * HALF])).reshape(4),
        jnp.stack([2 * HALF * (1 - upper), 2 * HALF * upper]),
    ]).astype(jnp.int32)
    weight = (batch_order[0, 0] >= 0).astype(F32)
    outs = work(place, weight, tiles, probe_wave, propagator, measured, half_tables())
    own, own_l, own_r, near, near_l, near_r, far, far_l, far_r, probe_term = outs

    ups = pairs_up(lax.axis_size("col"))

    def fold(middle, left, right):
        return middle + lax.ppermute(left, "col", flipped(ups)) + lax.ppermute(right, "col", ups)

    far = fold(far, far_l, far_r)
    near = fold(near, near_l, near_r) + lax.ppermute(far, "row", flipped(hops))
    own = fold(own, own_l, own_r) + lax.ppermute(near, "row", swap)
    return own, probe_block(probe_term)


def solution(mesh):
    placed = (
        P(None, None, "row", "col"),
        P(),
        P(),
        P("row", "col", None, None, None),
        P("row", "col", None, None),
        P("row", "col", None),
    )
    return jax.shard_map(
        per_device,
        mesh=mesh,
        in_specs=placed,
        out_specs=(P(None, None, "row", "col"), P(None, "row", "col")),
        check_vma=False,
    )
```

```python
import math

import jax
import jax.numpy as jnp
import numpy as np
from jax import lax
from jax.experimental import pallas as pl
from jax.experimental.pallas import tpu as pltpu
from jax.sharding import PartitionSpec as P

WIN = 256
HALF = 128
F32 = jnp.float32
BF16 = jnp.bfloat16


def frequency_order():
    return np.concatenate([np.arange(0, WIN, 2), np.arange(1, WIN, 2)])


def order_matrix():
    matrix = np.zeros((WIN, WIN), np.float32)
    matrix[np.arange(WIN), frequency_order()] = 1.0
    return jnp.asarray(matrix, BF16)


def half_tables():
    spots = np.arange(HALF)
    tables = []
    for parity in range(2):
        angles = 2.0 * math.pi * (np.outer(spots, 2 * spots + parity) % WIN) / WIN
        cosine, sine = (np.cos(angles) / 16.0, np.sin(angles) / 16.0)
        block = np.block([[cosine, -sine], [sine, cosine]])
        tables += [block, block.T]
    exact = np.stack(tables).astype(np.float32)
    high = exact.astype(jnp.bfloat16)
    low = (exact - high.astype(np.float32)).astype(jnp.bfloat16)
    return jnp.asarray(np.stack([high, low], axis=1))


def split(value):
    high = value.astype(BF16)
    return high, (value - high.astype(F32)).astype(BF16)


def dot(left, right):
    return jnp.dot(left, right, preferred_element_type=F32)


def right_mul(value, table_ref, index):
    high, low = split(value)
    table = table_ref[index, 0]
    return dot(high, table) + (dot(low, table) + dot(high, table_ref[index, 1]))


def left_mul(table_ref, index, value):
    high, low = split(value)
    table = table_ref[index, 0]
    return dot(table, high) + (dot(table, low) + dot(table_ref[index, 1], high))


def join(first, second, axis):
    return jnp.concatenate([first, second], axis=axis)


def halves(value, axis):
    if axis == 0:
        return value[:HALF], value[HALF:]
    return value[:, :HALF], value[:, HALF:]


def forward_axis(field, tables, axis):
    (re0, re1), (im0, im1) = (halves(field[0], axis), halves(field[1], axis))
    even = join(re0 + re1, im0 + im1, axis)
    odd = join(re0 - re1, im0 - im1, axis)
    if axis == 1:
        even, odd = (right_mul(even, tables, 0), right_mul(odd, tables, 2))
    else:
        even, odd = (left_mul(tables, 1, even), left_mul(tables, 3, odd))
    (re0, im0), (re1, im1) = (halves(even, axis), halves(odd, axis))
    return (join(re0, re1, axis), join(im0, im1, axis))


def inverse_axis(field, tables, axis):
    (re0, re1), (im0, im1) = (halves(field[0], axis), halves(field[1], axis))
    even = join(re0, im0, axis)
    odd = join(re1, im1, axis)
    if axis == 1:
        even, odd = (right_mul(even, tables, 1), right_mul(odd, tables, 3))
    else:
        even, odd = (left_mul(tables, 0, even), left_mul(tables, 2, odd))
    (re0, im0), (re1, im1) = (halves(even, axis), halves(odd, axis))
    return (join(re0 + re1, re0 - re1, axis), join(im0 + im1, im0 - im1, axis))


def forward(field, tables):
    return forward_axis(forward_axis(field, tables, 1), tables, 0)


def inverse(field, tables):
    return inverse_axis(inverse_axis(field, tables, 0), tables, 1)


def times(left, right):
    return (left[0] * right[0] - left[1] * right[1], left[0] * right[1] + left[1] * right[0])


def conj_times(left, right):
    return (left[0] * right[0] + left[1] * right[1], left[0] * right[1] - left[1] * right[0])


def cut_lanes(strip, shift):
    turned = [pltpu.roll(strip[:, k * HALF:(k + 1) * HALF], (HALF - shift) & (HALF - 1), 1) for k in range(3)]
    kept = lax.broadcasted_iota(jnp.int32, turned[0].shape, 1) < HALF - shift
    return jnp.concatenate([jnp.where(kept, turned[k], turned[k + 1]) for k in range(2)], axis=1)


def put_lanes(value, shift):
    turned = [pltpu.roll(value[:, k * HALF:(k + 1) * HALF], shift, 1) for k in range(2)]
    kept = lax.broadcasted_iota(jnp.int32, turned[0].shape, 1) >= shift
    return jnp.concatenate(
        [jnp.where(kept, turned[0], 0.0), jnp.where(kept, turned[1], turned[0]), jnp.where(kept, 0.0, turned[1])],
        axis=1,
    )


def cut_rows(strip, shift):
    groups = pltpu.roll(strip.reshape(WIN // 8 + 1, 8, strip.shape[1]), (8 - shift) & 7, 1)
    kept = lax.broadcasted_iota(jnp.int32, (WIN // 8, 8, strip.shape[1]), 1) < 8 - shift
    return jnp.where(kept, groups[:-1], groups[1:]).reshape(WIN, strip.shape[1])


def put_rows(value, shift):
    groups = pltpu.roll(value.reshape(WIN // 8, 8, value.shape[1]), shift, 1)
    none = jnp.zeros((1, 8, value.shape[1]), F32)
    kept = lax.broadcasted_iota(jnp.int32, (WIN // 8 + 1, 8, value.shape[1]), 1) >= shift
    here = jnp.concatenate([groups, none], axis=0)
    before = jnp.concatenate([none, groups], axis=0)
    return jnp.where(kept, here, before).reshape(WIN + 8, value.shape[1])


def work_kernel(place, weight, own, near, far, left, right, probe, propagator, intensity, tables,
                out_own, out_near, out_far, out_left, out_right, out_probe, extended, total, arrived, left_sem):
    tops = (HALF, pl.multiple_of(place[4], HALF), pl.multiple_of(place[5], HALF))

    def pieces(field, middle, before, after):
        for k in range(3):
            rows = pl.ds(tops[k], HALF)
            yield middle[k], field.at[:, :, rows, HALF:2 * HALF]
            yield before.at[k], field.at[:, :, rows, 0:HALF]
            yield after.at[k], field.at[:, :, rows, 2 * HALF:3 * HALF]

    loads = [
        pltpu.make_async_copy(source, target, arrived.at[n])
        for n, (source, target) in enumerate(pieces(extended, (own, near, far), left, right))
    ]
    for load in loads:
        load.start()
    total[...] = jnp.zeros(total.shape, F32)
    wave = (probe[0].astype(F32), probe[1].astype(F32))
    spread = (propagator[0], propagator[1])
    for load in loads:
        load.wait()
    for slot in range(2):
        row, col = (place[2 * slot], place[2 * slot + 1])
        low = row % 8
        base = pl.multiple_of(row - low, 8)

        def window(layer, part):
            strip = extended[layer, part, pl.ds(base, WIN + 8), :]
            return cut_rows(cut_lanes(strip, col), low)

        layer0 = (window(0, 0), window(0, 1))
        spectrum = forward(times(wave, layer0), tables)
        entering = inverse(times(spectrum, spread), tables)
        layer1 = (window(1, 0), window(1, 1))
        spectrum = forward(times(entering, layer1), tables)
        power = spectrum[0] * spectrum[0] + spectrum[1] * spectrum[1]
        misfit = weight[slot] * (power - intensity[slot])
        adjoint = inverse((misfit * spectrum[0], misfit * spectrum[1]), tables)
        term1 = conj_times(entering, adjoint)
        spectrum = forward(conj_times(layer1, adjoint), tables)
        adjoint = inverse(conj_times(spread, spectrum), tables)
        term0 = conj_times(wave, adjoint)
        upstream = conj_times(layer0, adjoint)
        blocks = out_probe.shape[0]
        for part in range(2):
            shared = upstream[part].reshape(blocks, WIN // blocks, WIN)
            if slot == 0:
                out_probe[:, part] = shared
            else:
                out_probe[:, part] += shared

        for layer, term in ((0, term0), (1, term1)):
            for part in range(2):
                total[layer, part, pl.ds(base, WIN + 8), :] += put_lanes(put_rows(term[part], low), col)
    stores = [
        pltpu.make_async_copy(source, target, left_sem.at[n])
        for n, (target, source) in enumerate(pieces(total, (out_own, out_near, out_far), out_left, out_right))
    ]
    for store in stores:
        store.start()
    for store in stores:
        store.wait()


def work(place, weight, tiles, probe, propagator, intensity, tables, blocks):
    vmem = pl.BlockSpec(memory_space=pltpu.VMEM)
    smem = pl.BlockSpec(memory_space=pltpu.SMEM)
    anywhere = pl.BlockSpec(memory_space=pl.ANY)
    tile = jax.ShapeDtypeStruct((2, 2, HALF, HALF), F32)
    triple = jax.ShapeDtypeStruct((3, 2, 2, HALF, HALF), F32)
    term = jax.ShapeDtypeStruct((blocks, 2, WIN // blocks, WIN), F32)
    return pl.pallas_call(
        work_kernel,
        out_shape=[tile] * 3 + [triple] * 2 + [term],
        in_specs=[smem, smem] + [anywhere] * 5 + [vmem] * 4,
        out_specs=[anywhere] * 5 + [vmem],
        scratch_shapes=[pltpu.VMEM((2, 2, 3 * HALF, 3 * HALF), F32)] * 2 + [pltpu.SemaphoreType.DMA((9,))] * 2,
        compiler_params=pltpu.CompilerParams(vmem_limit_bytes=48 * 1024 * 1024),
        cost_estimate=pl.CostEstimate(flops=10_000_000_000, bytes_accessed=8_000_000, transcendentals=0),
    )(place, weight, *tiles, probe, propagator, intensity, tables)


def pairs_up(count):
    return [(i, i + 1) for i in range(count - 1)]


def flipped(pairs):
    return [(j, i) for i, j in pairs]


def probe_rows(term):
    rows = lax.axis_size("row")
    groups = [[2 * k + half for k in range(rows // 2)] for half in range(2)]
    return lax.all_to_all(term, "row", 0, 0, tiled=True, axis_index_groups=groups)


def probe_block(spread):
    rows, cols = (lax.axis_size("row"), lax.axis_size("col"))
    pair = jnp.sum(spread, axis=0)
    size = pair.shape[1] // 2
    upper = lax.axis_index("row") % 2 == 1
    first, second = (pair[:, :size], pair[:, size:])
    swap = [(i, i ^ 1) for i in range(rows)]
    mine = jnp.where(upper, second, first) + lax.ppermute(jnp.where(upper, first, second), "row", swap)
    mine = mine.reshape(2, size, cols, WIN // cols).transpose(2, 0, 1, 3)
    return jnp.sum(lax.all_to_all(mine, "col", 0, 0, tiled=True), axis=0)


def per_device(object_slices, probe_wave, propagator_phase, intensity, centres, batch_order):
    rows = lax.axis_size("row")
    row, col = (lax.axis_index("row"), lax.axis_index("col"))
    hops = [(i, i + 2) for i in range(0, rows - 2, 2)] + [(i + 2, i) for i in range(1, rows - 2, 2)]
    swap = [(i, i ^ 1) for i in range(rows)]
    ups = pairs_up(lax.axis_size("col"))
    near = lax.ppermute(object_slices, "row", swap)
    far = lax.ppermute(near, "row", hops)
    stack = jnp.stack([object_slices, near, far])
    left = lax.ppermute(stack, "col", ups)
    right = lax.ppermute(stack, "col", flipped(ups))
    tiles = (object_slices, near, far, left, right)

    order = order_matrix()
    angles = dot(dot(order, propagator_phase).astype(BF16), order.T)
    propagator = jnp.stack([jnp.cos(angles), jnp.sin(angles)])
    middle = jnp.einsum("ab,sbc->sac", order, intensity[0, 0], preferred_element_type=F32).astype(BF16)
    measured = jnp.einsum("sac,dc->sad", middle, order, preferred_element_type=F32)
    upper = row % 2
    place = jnp.concatenate([
        (centres[0, 0] - jnp.stack([row * HALF, col * HALF])).reshape(4),
        jnp.stack([2 * HALF * (1 - upper), 2 * HALF * upper]),
    ]).astype(jnp.int32)
    weight = (batch_order[0, 0] >= 0).astype(F32)
    outs = work(place, weight, tiles, probe_wave, propagator, measured, half_tables(), rows // 2)
    own, near, far, left, right, probe_term = outs
    from_right = lax.ppermute(left, "col", flipped(ups))
    from_left = lax.ppermute(right, "col", ups)
    spread = probe_rows(probe_term)
    from_left, from_right, spread = lax.optimization_barrier((from_left, from_right, spread))
    far = far + from_left[2] + from_right[2]
    near = near + from_left[1] + from_right[1] + lax.ppermute(far, "row", flipped(hops))
    own = own + from_left[0] + from_right[0] + lax.ppermute(near, "row", swap)
    return own, probe_block(spread)


def solution(mesh):
    placed = (
        P(None, None, "row", "col"),
        P(),
        P(),
        P("row", "col", None, None, None),
        P("row", "col", None, None),
        P("row", "col", None),
    )
    return jax.shard_map(
        per_device,
        mesh=mesh,
        in_specs=placed,
        out_specs=(P(None, None, "row", "col"), P(None, "row", "col")),
        check_vma=False,
    )
```

```python
import math

import jax
import jax.numpy as jnp
import numpy as np
from jax import lax
from jax.experimental import pallas as pl
from jax.experimental.pallas import tpu as pltpu
from jax.sharding import PartitionSpec as P

WIN = 256
HALF = 128
F32 = jnp.float32
BF16 = jnp.bfloat16


def frequency_order():
    return np.concatenate([np.arange(0, WIN, 2), np.arange(1, WIN, 2)])


def order_matrix():
    matrix = np.zeros((WIN, WIN), np.float32)
    matrix[np.arange(WIN), frequency_order()] = 1.0
    return jnp.asarray(matrix, BF16)


def half_tables():
    spots = np.arange(HALF)
    tables = []
    for parity in range(2):
        angles = 2.0 * math.pi * (np.outer(spots, 2 * spots + parity) % WIN) / WIN
        cosine, sine = (np.cos(angles) / 16.0, np.sin(angles) / 16.0)
        block = np.block([[cosine, -sine], [sine, cosine]])
        tables += [block, block.T]
    exact = np.stack(tables).astype(np.float32)
    high = exact.astype(jnp.bfloat16)
    low = (exact - high.astype(np.float32)).astype(jnp.bfloat16)
    return jnp.asarray(np.stack([high, low], axis=1))


def split(value):
    high = value.astype(BF16)
    return high, (value - high.astype(F32)).astype(BF16)


def dot(left, right):
    return jnp.dot(left, right, preferred_element_type=F32)


def right_mul(value, table_ref, index):
    high, low = split(value)
    table = table_ref[index, 0]
    return dot(high, table) + (dot(low, table) + dot(high, table_ref[index, 1]))


def left_mul(table_ref, index, value):
    high, low = split(value)
    table = table_ref[index, 0]
    return dot(table, high) + (dot(table, low) + dot(table_ref[index, 1], high))


def join(first, second, axis):
    return jnp.concatenate([first, second], axis=axis)


def halves(value, axis):
    if axis == 0:
        return value[:HALF], value[HALF:]
    return value[:, :HALF], value[:, HALF:]


def forward_axis(field, tables, axis):
    (re0, re1), (im0, im1) = (halves(field[0], axis), halves(field[1], axis))
    even = join(re0 + re1, im0 + im1, axis)
    odd = join(re0 - re1, im0 - im1, axis)
    if axis == 1:
        even, odd = (right_mul(even, tables, 0), right_mul(odd, tables, 2))
    else:
        even, odd = (left_mul(tables, 1, even), left_mul(tables, 3, odd))
    (re0, im0), (re1, im1) = (halves(even, axis), halves(odd, axis))
    return (join(re0, re1, axis), join(im0, im1, axis))


def inverse_axis(field, tables, axis):
    (re0, re1), (im0, im1) = (halves(field[0], axis), halves(field[1], axis))
    even = join(re0, im0, axis)
    odd = join(re1, im1, axis)
    if axis == 1:
        even, odd = (right_mul(even, tables, 1), right_mul(odd, tables, 3))
    else:
        even, odd = (left_mul(tables, 0, even), left_mul(tables, 2, odd))
    (re0, im0), (re1, im1) = (halves(even, axis), halves(odd, axis))
    return (join(re0 + re1, re0 - re1, axis), join(im0 + im1, im0 - im1, axis))


def forward(field, tables):
    return forward_axis(forward_axis(field, tables, 1), tables, 0)


def inverse(field, tables):
    return inverse_axis(inverse_axis(field, tables, 0), tables, 1)


def times(left, right):
    return (left[0] * right[0] - left[1] * right[1], left[0] * right[1] + left[1] * right[0])


def conj_times(left, right):
    return (left[0] * right[0] + left[1] * right[1], left[0] * right[1] - left[1] * right[0])


def cut_lanes(strip, shift):
    turned = [pltpu.roll(strip[:, k * HALF:(k + 1) * HALF], (HALF - shift) & (HALF - 1), 1) for k in range(3)]
    kept = lax.broadcasted_iota(jnp.int32, turned[0].shape, 1) < HALF - shift
    return jnp.concatenate([jnp.where(kept, turned[k], turned[k + 1]) for k in range(2)], axis=1)


def put_lanes(value, shift):
    turned = [pltpu.roll(value[:, k * HALF:(k + 1) * HALF], shift, 1) for k in range(2)]
    kept = lax.broadcasted_iota(jnp.int32, turned[0].shape, 1) >= shift
    return jnp.concatenate(
        [jnp.where(kept, turned[0], 0.0), jnp.where(kept, turned[1], turned[0]), jnp.where(kept, 0.0, turned[1])],
        axis=1,
    )


def cut_rows(strip, shift):
    groups = pltpu.roll(strip.reshape(WIN // 8 + 1, 8, strip.shape[1]), (8 - shift) & 7, 1)
    kept = lax.broadcasted_iota(jnp.int32, (WIN // 8, 8, strip.shape[1]), 1) < 8 - shift
    return jnp.where(kept, groups[:-1], groups[1:]).reshape(WIN, strip.shape[1])


def put_rows(value, shift):
    groups = pltpu.roll(value.reshape(WIN // 8, 8, value.shape[1]), shift, 1)
    none = jnp.zeros((1, 8, value.shape[1]), F32)
    kept = lax.broadcasted_iota(jnp.int32, (WIN // 8 + 1, 8, value.shape[1]), 1) >= shift
    here = jnp.concatenate([groups, none], axis=0)
    before = jnp.concatenate([none, groups], axis=0)
    return jnp.where(kept, here, before).reshape(WIN + 8, value.shape[1])


def pieces(place, field, middle, sibling, other):
    tops = (HALF, pl.multiple_of(place[4], HALF), pl.multiple_of(place[5], HALF))
    for k in range(3):
        rows = pl.ds(tops[k], HALF)
        yield middle[k], field.at[:, rows, HALF:2 * HALF]
        yield sibling[k], field.at[:, rows, pl.ds(pl.multiple_of(place[6], HALF), HALF)]
        yield other[k], field.at[:, rows, pl.ds(pl.multiple_of(place[7], HALF), HALF)]


def spot(place, slot):
    row, col = (place[2 * slot], place[2 * slot + 1])
    low = row % 8
    return pl.multiple_of(row - low, 8), low, col


def window(field, place, slot):
    base, low, col = spot(place, slot)
    strips = [field[part, pl.ds(base, WIN + 8), :] for part in range(2)]
    return tuple(cut_rows(cut_lanes(strip, col), low) for strip in strips)


def add_window(field, place, slot, term):
    base, low, col = spot(place, slot)
    for part in range(2):
        field[part, pl.ds(base, WIN + 8), :] += put_lanes(put_rows(term[part], low), col)


def assemble(place, field, layer, own, near, far, sibling, other, arrived):
    middle = [tile.at[layer] for tile in (own, near, far)]
    parts = pieces(place, field, middle, [sibling.at[k] for k in range(3)], [other.at[k] for k in range(3)])
    return [pltpu.make_async_copy(a, b, arrived.at[n]) for n, (a, b) in enumerate(parts)]


def front_kernel(place, own, near, far, sibling, other, probe, propagator, tables, out_wave, out_layer, field, arrived):
    loads = assemble(place, field, 0, own, near, far, sibling, other, arrived)
    for load in loads:
        load.start()
    wave = (probe[0].astype(F32), probe[1].astype(F32))
    spread = (propagator[0], propagator[1])
    for load in loads:
        load.wait()
    for slot in range(2):
        layer = window(field, place, slot)
        spectrum = forward(times(wave, layer), tables)
        entering = inverse(times(spectrum, spread), tables)
        for part in range(2):
            out_layer[slot, part] = layer[part]
            out_wave[slot, part] = entering[part]


def back_kernel(place, weight, own, near, far, sibling, other, waves, layers, probe, propagator, intensity, tables,
                out_own, out_near, out_far, out_sibling, out_other, out_probe, field, total0, total1, kept, arrived, left_sem):
    loads = assemble(place, field, 1, own, near, far, sibling, other, arrived)
    for load in loads:
        load.start()
    totals = (total0, total1)

    def stores(layer):
        middle = [tile.at[layer] for tile in (out_own, out_near, out_far)]
        sides = [[side.at[k, layer] for k in range(3)] for side in (out_sibling, out_other)]
        parts = pieces(place, totals[layer], middle, *sides)
        return [pltpu.make_async_copy(b, a, left_sem.at[layer, n]) for n, (a, b) in enumerate(parts)]

    for total in totals:
        total[...] = jnp.zeros(total.shape, F32)
    spread = (propagator[0], propagator[1])
    for load in loads:
        load.wait()
    for slot in range(2):
        entering = (waves[slot, 0], waves[slot, 1])
        layer = window(field, place, slot)
        spectrum = forward(times(entering, layer), tables)
        power = spectrum[0] * spectrum[0] + spectrum[1] * spectrum[1]
        misfit = weight[slot] * (power - intensity[slot])
        adjoint = inverse((misfit * spectrum[0], misfit * spectrum[1]), tables)
        add_window(total1, place, slot, conj_times(entering, adjoint))
        upstream = conj_times(layer, adjoint)
        for part in range(2):
            kept[slot, part] = upstream[part]
    for store in stores(1):
        store.start()
    wave = (probe[0].astype(F32), probe[1].astype(F32))
    for slot in range(2):
        spectrum = forward((kept[slot, 0], kept[slot, 1]), tables)
        adjoint = inverse(conj_times(spread, spectrum), tables)
        add_window(total0, place, slot, conj_times(wave, adjoint))
        upstream = conj_times((layers[slot, 0], layers[slot, 1]), adjoint)
        blocks = out_probe.shape[0]
        for part in range(2):
            shared = upstream[part].reshape(blocks, WIN // blocks, WIN)
            if slot == 0:
                out_probe[:, part] = shared
            else:
                out_probe[:, part] += shared
    for store in stores(0):
        store.start()
    for layer in range(2):
        for store in stores(layer):
            store.wait()


VMEM = pl.BlockSpec(memory_space=pltpu.VMEM)
SMEM = pl.BlockSpec(memory_space=pltpu.SMEM)
ANYWHERE = pl.BlockSpec(memory_space=pl.ANY)


def shaped(*shape):
    return jax.ShapeDtypeStruct(shape, F32)


def call(kernel, out_shape, in_specs, out_specs, scratch_shapes, flops):
    return pl.pallas_call(
        kernel,
        out_shape=out_shape,
        in_specs=in_specs,
        out_specs=out_specs,
        scratch_shapes=scratch_shapes,
        compiler_params=pltpu.CompilerParams(vmem_limit_bytes=24 * 1024 * 1024),
        cost_estimate=pl.CostEstimate(flops=flops, bytes_accessed=4_000_000, transcendentals=0),
    )


def front(place, tiles, probe, propagator, tables):
    return call(
        front_kernel,
        [shaped(2, 2, WIN, WIN)] * 2,
        [SMEM] + [ANYWHERE] * 5 + [VMEM] * 3,
        [VMEM] * 2,
        [pltpu.VMEM((2, 3 * HALF, 3 * HALF), F32), pltpu.SemaphoreType.DMA((9,))],
        3_300_000_000,
    )(place, *tiles, probe, propagator, tables)


def back(place, weight, tiles, waves, layers, probe, propagator, intensity, tables, blocks):
    return call(
        back_kernel,
        [shaped(2, 2, HALF, HALF)] * 3 + [shaped(3, 2, 2, HALF, HALF)] * 2 + [shaped(blocks, 2, WIN // blocks, WIN)],
        [SMEM] * 2 + [ANYWHERE] * 5 + [VMEM] * 6,
        [ANYWHERE] * 5 + [VMEM],
        [pltpu.VMEM((2, 3 * HALF, 3 * HALF), F32)] * 3
        + [pltpu.VMEM((2, 2, WIN, WIN), F32), pltpu.SemaphoreType.DMA((9,)), pltpu.SemaphoreType.DMA((2, 9))],
        6_600_000_000,
    )(place, weight, *tiles, waves, layers, probe, propagator, intensity, tables)


def flipped(pairs):
    return [(j, i) for i, j in pairs]


def sides(value):
    cols = lax.axis_size("col")
    inner = [(i, i + 1) for i in range(1, cols - 1, 2)]
    other = lax.ppermute(value, "col", inner + flipped(inner))
    return lax.ppermute(value, "col", [(i, i ^ 1) for i in range(cols)]), other


def probe_rows(term):
    rows = lax.axis_size("row")
    groups = [[2 * k + half for k in range(rows // 2)] for half in range(2)]
    return lax.all_to_all(term, "row", 0, 0, tiled=True, axis_index_groups=groups)


def probe_block(pair):
    rows, cols = (lax.axis_size("row"), lax.axis_size("col"))
    size, width = (WIN // rows, WIN // cols)
    parts = pair.reshape(2, 2, size, cols, width).transpose(1, 3, 0, 2, 4).reshape(2 * cols, 2, size, width)
    groups = [[(2 * k + half) * cols + c for half in range(2) for c in range(cols)] for k in range(rows // 2)]
    gathered = lax.all_to_all(parts, ("row", "col"), 0, 0, tiled=True, axis_index_groups=groups)
    return jnp.sum(gathered, axis=0)


def per_device(object_slices, probe_wave, propagator_phase, intensity, centres, batch_order):
    rows = lax.axis_size("row")
    row, col = (lax.axis_index("row"), lax.axis_index("col"))
    hops = [(i, i + 2) for i in range(0, rows - 2, 2)] + [(i + 2, i) for i in range(1, rows - 2, 2)]
    swap = [(i, i ^ 1) for i in range(rows)]
    near = lax.ppermute(object_slices, "row", swap)
    far = lax.ppermute(near, "row", hops)
    stacks = lax.optimization_barrier([jnp.stack([object_slices[k], near[k], near[k]]) for k in range(2)])
    sent = [lax.dynamic_update_slice(stacks[k], far[k][None], (2, 0, 0, 0)) for k in range(2)]
    sides0, sides1 = (sides(sent[0]), sides(sent[1]))

    order = order_matrix()
    angles = dot(dot(order, propagator_phase).astype(BF16), order.T)
    propagator = jnp.stack([jnp.cos(angles), jnp.sin(angles)])
    middle = jnp.einsum("ab,sbc->sac", order, intensity[0, 0], preferred_element_type=F32).astype(BF16)
    measured = jnp.einsum("sac,dc->sad", middle, order, preferred_element_type=F32)
    upper, odd = (row % 2, col % 2)
    place = jnp.concatenate([
        (centres[0, 0] - jnp.stack([row * HALF, col * HALF])).reshape(4),
        2 * HALF * jnp.stack([1 - upper, upper, 1 - odd, odd]),
    ]).astype(jnp.int32)
    weight = (batch_order[0, 0] >= 0).astype(F32)
    tables = half_tables()
    tiles = (object_slices, near, far)
    waves, layers = front(place, tiles + sides0, probe_wave, propagator, tables)
    outs = back(place, weight, tiles + sides1, waves, layers, probe_wave, propagator, measured, tables, rows // 2)
    own, near, far, to_sibling, to_other, probe_term = outs
    cols = lax.axis_size("col")
    inner = [(i, i + 1) for i in range(1, cols - 1, 2)]
    other = lax.ppermute(to_other, "col", inner + flipped(inner))
    sibling = lax.ppermute(to_sibling, "col", [(i, i ^ 1) for i in range(cols)])
    spread = probe_rows(probe_term)
    sibling, other, spread = lax.optimization_barrier((sibling, other, spread))
    far = lax.ppermute(far + sibling[2] + other[2], "row", flipped(hops))
    far, pair = lax.optimization_barrier((far, jnp.sum(spread, axis=0)))
    near = near + sibling[1] + other[1] + far
    own = own + sibling[0] + other[0] + lax.ppermute(near, "row", swap)
    return own, probe_block(pair)


def solution(mesh):
    placed = (
        P(None, None, "row", "col"),
        P(),
        P(),
        P("row", "col", None, None, None),
        P("row", "col", None, None),
        P("row", "col", None),
    )
    return jax.shard_map(
        per_device,
        mesh=mesh,
        in_specs=placed,
        out_specs=(P(None, None, "row", "col"), P(None, "row", "col")),
        check_vma=False,
    )
```

```python
import math

import jax
import jax.numpy as jnp
import numpy as np
from jax import lax
from jax.experimental import pallas as pl
from jax.experimental.pallas import tpu as pltpu
from jax.sharding import PartitionSpec as P

WIN = 256
HALF = 128
F32 = jnp.float32
BF16 = jnp.bfloat16


def frequency_order():
    return np.concatenate([np.arange(0, WIN, 2), np.arange(1, WIN, 2)])


def order_matrix():
    matrix = np.zeros((WIN, WIN), np.float32)
    matrix[np.arange(WIN), frequency_order()] = 1.0
    return jnp.asarray(matrix, BF16)


def half_tables():
    spots = np.arange(HALF)
    tables = []
    for parity in range(2):
        angles = 2.0 * math.pi * (np.outer(spots, 2 * spots + parity) % WIN) / WIN
        cosine, sine = (np.cos(angles) / 16.0, np.sin(angles) / 16.0)
        block = np.block([[cosine, -sine], [sine, cosine]])
        tables += [block, block.T]
    exact = np.stack(tables).astype(np.float32)
    high = exact.astype(jnp.bfloat16)
    low = (exact - high.astype(np.float32)).astype(jnp.bfloat16)
    return jnp.asarray(np.stack([high, low], axis=1))


def split(value):
    high = value.astype(BF16)
    return high, (value - high.astype(F32)).astype(BF16)


def dot(left, right):
    return jnp.dot(left, right, preferred_element_type=F32)


def right_mul(value, table_ref, index):
    high, low = split(value)
    table = table_ref[index, 0]
    both = dot(join(high, low, 0), table)
    size = value.shape[0]
    return both[:size] + (both[size:] + dot(high, table_ref[index, 1]))


def left_mul(table_ref, index, value):
    high, low = split(value)
    table = table_ref[index, 0]
    both = dot(join(table, table_ref[index, 1], 0), high)
    size = table.shape[0]
    return both[:size] + (dot(table, low) + both[size:])


def join(first, second, axis):
    return jnp.concatenate([first, second], axis=axis)


def halves(value, axis):
    if axis == 0:
        return value[:HALF], value[HALF:]
    return value[:, :HALF], value[:, HALF:]


def mul_all(values, tables, index, axis):
    if axis == 1:
        out = right_mul(jnp.concatenate(values, axis=0), tables, index)
        return [out[n * WIN:(n + 1) * WIN] for n in range(len(values))]
    return [left_mul(tables, index, value) for value in values]


def forward_axis(fields, tables, axis):
    evens, odds = ([], [])
    for field in fields:
        (re0, re1), (im0, im1) = (halves(field[0], axis), halves(field[1], axis))
        evens.append(join(re0 + re1, im0 + im1, axis))
        odds.append(join(re0 - re1, im0 - im1, axis))
    evens = mul_all(evens, tables, 0 if axis == 1 else 1, axis)
    odds = mul_all(odds, tables, 2 if axis == 1 else 3, axis)
    outs = []
    for even, odd in zip(evens, odds):
        (re0, im0), (re1, im1) = (halves(even, axis), halves(odd, axis))
        outs.append((join(re0, re1, axis), join(im0, im1, axis)))
    return outs


def inverse_axis(fields, tables, axis):
    evens, odds = ([], [])
    for field in fields:
        (re0, re1), (im0, im1) = (halves(field[0], axis), halves(field[1], axis))
        evens.append(join(re0, im0, axis))
        odds.append(join(re1, im1, axis))
    evens = mul_all(evens, tables, 1 if axis == 1 else 0, axis)
    odds = mul_all(odds, tables, 3 if axis == 1 else 2, axis)
    outs = []
    for even, odd in zip(evens, odds):
        (re0, im0), (re1, im1) = (halves(even, axis), halves(odd, axis))
        outs.append((join(re0 + re1, re0 - re1, axis), join(im0 + im1, im0 - im1, axis)))
    return outs


def forward(fields, tables):
    return forward_axis(forward_axis(fields, tables, 1), tables, 0)


def inverse(fields, tables):
    return inverse_axis(inverse_axis(fields, tables, 0), tables, 1)


def times(left, right):
    return (left[0] * right[0] - left[1] * right[1], left[0] * right[1] + left[1] * right[0])


def conj_times(left, right):
    return (left[0] * right[0] + left[1] * right[1], left[0] * right[1] - left[1] * right[0])


def cut_lanes(strip, shift):
    turned = [pltpu.roll(strip[:, k * HALF:(k + 1) * HALF], (HALF - shift) & (HALF - 1), 1) for k in range(3)]
    kept = lax.broadcasted_iota(jnp.int32, turned[0].shape, 1) < HALF - shift
    return jnp.concatenate([jnp.where(kept, turned[k], turned[k + 1]) for k in range(2)], axis=1)


def put_lanes(value, shift):
    turned = [pltpu.roll(value[:, k * HALF:(k + 1) * HALF], shift, 1) for k in range(2)]
    kept = lax.broadcasted_iota(jnp.int32, turned[0].shape, 1) >= shift
    return jnp.concatenate(
        [jnp.where(kept, turned[0], 0.0), jnp.where(kept, turned[1], turned[0]), jnp.where(kept, 0.0, turned[1])],
        axis=1,
    )


def cut_rows(strip, shift):
    groups = pltpu.roll(strip.reshape(WIN // 8 + 1, 8, strip.shape[1]), (8 - shift) & 7, 1)
    kept = lax.broadcasted_iota(jnp.int32, (WIN // 8, 8, strip.shape[1]), 1) < 8 - shift
    return jnp.where(kept, groups[:-1], groups[1:]).reshape(WIN, strip.shape[1])


def put_rows(value, shift):
    groups = pltpu.roll(value.reshape(WIN // 8, 8, value.shape[1]), shift, 1)
    none = jnp.zeros((1, 8, value.shape[1]), F32)
    kept = lax.broadcasted_iota(jnp.int32, (WIN // 8 + 1, 8, value.shape[1]), 1) >= shift
    here = jnp.concatenate([groups, none], axis=0)
    before = jnp.concatenate([none, groups], axis=0)
    return jnp.where(kept, here, before).reshape(WIN + 8, value.shape[1])


def pieces(place, field, middle, sibling, other):
    tops = (HALF, pl.multiple_of(place[4], HALF), pl.multiple_of(place[5], HALF))
    for k in range(3):
        rows = pl.ds(tops[k], HALF)
        yield middle[k], field.at[:, rows, HALF:2 * HALF]
        yield sibling[k], field.at[:, rows, pl.ds(pl.multiple_of(place[6], HALF), HALF)]
        yield other[k], field.at[:, rows, pl.ds(pl.multiple_of(place[7], HALF), HALF)]


def spot(place, slot):
    row, col = (place[2 * slot], place[2 * slot + 1])
    low = row % 8
    return pl.multiple_of(row - low, 8), low, col


def window(field, place, slot):
    base, low, col = spot(place, slot)
    strips = [field[part, pl.ds(base, WIN + 8), :] for part in range(2)]
    return tuple(cut_rows(cut_lanes(strip, col), low) for strip in strips)


def add_window(field, place, slot, term):
    base, low, col = spot(place, slot)
    for part in range(2):
        field[part, pl.ds(base, WIN + 8), :] += put_lanes(put_rows(term[part], low), col)


def assemble(place, field, layer, own, near, far, sibling, other, arrived):
    middle = [tile.at[layer] for tile in (own, near, far)]
    parts = pieces(place, field, middle, [sibling.at[k] for k in range(3)], [other.at[k] for k in range(3)])
    return [pltpu.make_async_copy(a, b, arrived.at[n]) for n, (a, b) in enumerate(parts)]


def front_kernel(place, own, near, far, sibling, other, probe, propagator, tables, out_wave, out_layer, field, arrived):
    loads = assemble(place, field, 0, own, near, far, sibling, other, arrived)
    for load in loads:
        load.start()
    wave = (probe[0].astype(F32), probe[1].astype(F32))
    spread = (propagator[0], propagator[1])
    for load in loads:
        load.wait()
    layers = [window(field, place, slot) for slot in range(2)]
    spectra = forward([times(wave, layer) for layer in layers], tables)
    entering = inverse([times(spectrum, spread) for spectrum in spectra], tables)
    for slot in range(2):
        for part in range(2):
            out_layer[slot, part] = layers[slot][part]
            out_wave[slot, part] = entering[slot][part]


def back_kernel(place, weight, own, near, far, sibling, other, waves, layers, probe, propagator, intensity, tables,
                out_own, out_near, out_far, out_sibling, out_other, out_probe, field, total0, total1, kept, arrived, left_sem):
    loads = assemble(place, field, 1, own, near, far, sibling, other, arrived)
    for load in loads:
        load.start()
    totals = (total0, total1)

    def stores(layer):
        middle = [tile.at[layer] for tile in (out_own, out_near, out_far)]
        sides = [[side.at[k, layer] for k in range(3)] for side in (out_sibling, out_other)]
        parts = pieces(place, totals[layer], middle, *sides)
        return [pltpu.make_async_copy(b, a, left_sem.at[layer, n]) for n, (a, b) in enumerate(parts)]

    for total in totals:
        total[...] = jnp.zeros(total.shape, F32)
    spread = (propagator[0], propagator[1])
    for load in loads:
        load.wait()
    two = range(2)
    spectra = forward([times((waves[slot, 0], waves[slot, 1]), window(field, place, slot)) for slot in two], tables)
    fields = []
    for slot in two:
        spectrum = spectra[slot]
        power = spectrum[0] * spectrum[0] + spectrum[1] * spectrum[1]
        misfit = weight[slot] * (power - intensity[slot])
        fields.append((misfit * spectrum[0], misfit * spectrum[1]))
    adjoint = inverse(fields, tables)
    for slot in two:
        add_window(total1, place, slot, conj_times((waves[slot, 0], waves[slot, 1]), adjoint[slot]))
        upstream = conj_times(window(field, place, slot), adjoint[slot])
        for part in range(2):
            kept[slot, part] = upstream[part]
    for store in stores(1):
        store.start()
    wave = (probe[0].astype(F32), probe[1].astype(F32))
    spectra = forward([(kept[slot, 0], kept[slot, 1]) for slot in two], tables)
    adjoint = inverse([conj_times(spread, spectrum) for spectrum in spectra], tables)
    for slot in two:
        add_window(total0, place, slot, conj_times(wave, adjoint[slot]))
    for store in stores(0):
        store.start()
    upstream = [conj_times((layers[slot, 0], layers[slot, 1]), adjoint[slot]) for slot in two]
    blocks = out_probe.shape[0]
    for part in range(2):
        out_probe[:, part] = (upstream[0][part] + upstream[1][part]).reshape(blocks, WIN // blocks, WIN)
    for layer in range(2):
        for store in stores(layer):
            store.wait()


VMEM = pl.BlockSpec(memory_space=pltpu.VMEM)
SMEM = pl.BlockSpec(memory_space=pltpu.SMEM)
ANYWHERE = pl.BlockSpec(memory_space=pl.ANY)


def shaped(*shape):
    return jax.ShapeDtypeStruct(shape, F32)


def call(kernel, out_shape, in_specs, out_specs, scratch_shapes, flops):
    return pl.pallas_call(
        kernel,
        out_shape=out_shape,
        in_specs=in_specs,
        out_specs=out_specs,
        scratch_shapes=scratch_shapes,
        compiler_params=pltpu.CompilerParams(vmem_limit_bytes=24 * 1024 * 1024),
        cost_estimate=pl.CostEstimate(flops=flops, bytes_accessed=4_000_000, transcendentals=0),
    )


def front(place, tiles, probe, propagator, tables):
    return call(
        front_kernel,
        [shaped(2, 2, WIN, WIN)] * 2,
        [SMEM] + [ANYWHERE] * 5 + [VMEM] * 3,
        [VMEM] * 2,
        [pltpu.VMEM((2, 3 * HALF, 3 * HALF), F32), pltpu.SemaphoreType.DMA((9,))],
        3_300_000_000,
    )(place, *tiles, probe, propagator, tables)


def back(place, weight, tiles, waves, layers, probe, propagator, intensity, tables, blocks):
    return call(
        back_kernel,
        [shaped(2, 2, HALF, HALF)] * 3 + [shaped(3, 2, 2, HALF, HALF)] * 2 + [shaped(blocks, 2, WIN // blocks, WIN)],
        [SMEM] * 2 + [ANYWHERE] * 5 + [VMEM] * 6,
        [ANYWHERE] * 5 + [VMEM],
        [pltpu.VMEM((2, 3 * HALF, 3 * HALF), F32)] * 3
        + [pltpu.VMEM((2, 2, WIN, WIN), F32), pltpu.SemaphoreType.DMA((9,)), pltpu.SemaphoreType.DMA((2, 9))],
        6_600_000_000,
    )(place, weight, *tiles, waves, layers, probe, propagator, intensity, tables)


def flipped(pairs):
    return [(j, i) for i, j in pairs]


def sides(value):
    cols = lax.axis_size("col")
    inner = [(i, i + 1) for i in range(1, cols - 1, 2)]
    other = lax.ppermute(value, "col", inner + flipped(inner))
    return lax.ppermute(value, "col", [(i, i ^ 1) for i in range(cols)]), other


def probe_rows(term):
    rows = lax.axis_size("row")
    groups = [[2 * k + half for k in range(rows // 2)] for half in range(2)]
    return lax.all_to_all(term, "row", 0, 0, tiled=True, axis_index_groups=groups)


def probe_block(pair, own):
    rows, cols = (lax.axis_size("row"), lax.axis_size("col"))
    size, width = (WIN // rows, WIN // cols)
    parts = pair.reshape(2, 2, size, cols, width).transpose(1, 3, 0, 2, 4).reshape(2 * cols, 2, size * width)
    groups = [[(2 * k + half) * cols + c for half in range(2) for c in range(cols)] for k in range(rows // 2)]
    gathered = lax.all_to_all(parts, ("row", "col"), 0, 0, tiled=True, axis_index_groups=groups)
    own, gathered = lax.optimization_barrier((own, gathered))
    return own, jnp.sum(gathered, axis=0).reshape(2, size, width)


def per_device(object_slices, probe_wave, propagator_phase, intensity, centres, batch_order):
    rows = lax.axis_size("row")
    row, col = (lax.axis_index("row"), lax.axis_index("col"))
    hops = [(i, i + 2) for i in range(0, rows - 2, 2)] + [(i + 2, i) for i in range(1, rows - 2, 2)]
    swap = [(i, i ^ 1) for i in range(rows)]
    near = lax.ppermute(object_slices, "row", swap)
    far = lax.ppermute(near, "row", hops)
    stacks = lax.optimization_barrier([jnp.stack([object_slices[k], near[k], near[k]]) for k in range(2)])
    sent = [lax.dynamic_update_slice(stacks[k], far[k][None], (2, 0, 0, 0)) for k in range(2)]
    sides0, sides1 = (sides(sent[0]), sides(sent[1]))

    order = order_matrix()
    angles = dot(dot(order, propagator_phase).astype(BF16), order.T)
    propagator = jnp.stack([jnp.cos(angles), jnp.sin(angles)])
    middle = jnp.einsum("ab,sbc->sac", order, intensity[0, 0], preferred_element_type=F32).astype(BF16)
    measured = jnp.einsum("sac,dc->sad", middle, order, preferred_element_type=F32)
    upper, odd = (row % 2, col % 2)
    place = jnp.concatenate([
        (centres[0, 0] - jnp.stack([row * HALF, col * HALF])).reshape(4),
        2 * HALF * jnp.stack([1 - upper, upper, 1 - odd, odd]),
    ]).astype(jnp.int32)
    weight = (batch_order[0, 0] >= 0).astype(F32)
    tables = half_tables()
    tiles = (object_slices, near, far)
    waves, layers = front(place, tiles + sides0, probe_wave, propagator, tables)
    outs = back(place, weight, tiles + sides1, waves, layers, probe_wave, propagator, measured, tables, rows // 2)
    own, near, far, to_sibling, to_other, probe_term = outs
    cols = lax.axis_size("col")
    inner = [(i, i + 1) for i in range(1, cols - 1, 2)]
    other = lax.ppermute(to_other, "col", inner + flipped(inner))
    sibling = lax.ppermute(to_sibling, "col", [(i, i ^ 1) for i in range(cols)])
    spread = probe_rows(probe_term)
    far = lax.ppermute(far + sibling[2] + other[2], "row", flipped(hops))
    pair = jnp.sum(spread, axis=0)
    near = near + sibling[1] + other[1] + far
    own = own + sibling[0] + other[0] + lax.ppermute(near, "row", swap)
    return probe_block(pair, own)


def solution(mesh):
    placed = (
        P(None, None, "row", "col"),
        P(),
        P(),
        P("row", "col", None, None, None),
        P("row", "col", None, None),
        P("row", "col", None),
    )
    return jax.shard_map(
        per_device,
        mesh=mesh,
        in_specs=placed,
        out_specs=(P(None, None, "row", "col"), P(None, "row", "col")),
        check_vma=False,
    )
```

```python
import math

import jax
import jax.numpy as jnp
import numpy as np
from jax import lax
from jax.experimental import pallas as pl
from jax.experimental.pallas import tpu as pltpu
from jax.sharding import PartitionSpec as P

WIN = 256
HALF = 128
F32 = jnp.float32
BF16 = jnp.bfloat16


def frequency_order():
    return np.concatenate([np.arange(0, WIN, 2), np.arange(1, WIN, 2)])


def order_matrix():
    matrix = np.zeros((WIN, WIN), np.float32)
    matrix[np.arange(WIN), frequency_order()] = 1.0
    return jnp.asarray(matrix, BF16)


def half_tables():
    spots = np.arange(HALF)
    tables = []
    for parity in range(2):
        angles = 2.0 * math.pi * (np.outer(spots, 2 * spots + parity) % WIN) / WIN
        cosine, sine = (np.cos(angles) / 16.0, np.sin(angles) / 16.0)
        block = np.block([[cosine, -sine], [sine, cosine]])
        tables += [block, block.T]
    exact = np.stack(tables).astype(np.float32)
    high = exact.astype(jnp.bfloat16)
    low = (exact - high.astype(np.float32)).astype(jnp.bfloat16)
    return jnp.asarray(np.stack([high, low], axis=1))


def split(value):
    high = value.astype(BF16)
    return high, (value - high.astype(F32)).astype(BF16)


def dot(left, right):
    return jnp.dot(left, right, preferred_element_type=F32)


def right_mul(value, table_ref, index):
    high, low = split(value)
    table = table_ref[index, 0]
    both = dot(join(high, low, 0), table)
    size = value.shape[0]
    return both[:size] + (both[size:] + dot(high, table_ref[index, 1]))


def left_mul(table_ref, index, value):
    high, low = split(value)
    table = table_ref[index, 0]
    both = dot(join(table, table_ref[index, 1], 0), high)
    size = table.shape[0]
    return both[:size] + (dot(table, low) + both[size:])


def join(first, second, axis):
    return jnp.concatenate([first, second], axis=axis)


def halves(value, axis):
    if axis == 0:
        return value[:HALF], value[HALF:]
    return value[:, :HALF], value[:, HALF:]


def mul_all(values, tables, index, axis):
    if axis == 1:
        out = right_mul(jnp.concatenate(values, axis=0), tables, index)
        return [out[n * WIN:(n + 1) * WIN] for n in range(len(values))]
    return [left_mul(tables, index, value) for value in values]


def forward_axis(fields, tables, axis):
    evens, odds = ([], [])
    for field in fields:
        (re0, re1), (im0, im1) = (halves(field[0], axis), halves(field[1], axis))
        evens.append(join(re0 + re1, im0 + im1, axis))
        odds.append(join(re0 - re1, im0 - im1, axis))
    evens = mul_all(evens, tables, 0 if axis == 1 else 1, axis)
    odds = mul_all(odds, tables, 2 if axis == 1 else 3, axis)
    outs = []
    for even, odd in zip(evens, odds):
        (re0, im0), (re1, im1) = (halves(even, axis), halves(odd, axis))
        outs.append((join(re0, re1, axis), join(im0, im1, axis)))
    return outs


def inverse_axis(fields, tables, axis):
    evens, odds = ([], [])
    for field in fields:
        (re0, re1), (im0, im1) = (halves(field[0], axis), halves(field[1], axis))
        evens.append(join(re0, im0, axis))
        odds.append(join(re1, im1, axis))
    evens = mul_all(evens, tables, 1 if axis == 1 else 0, axis)
    odds = mul_all(odds, tables, 3 if axis == 1 else 2, axis)
    outs = []
    for even, odd in zip(evens, odds):
        (re0, im0), (re1, im1) = (halves(even, axis), halves(odd, axis))
        outs.append((join(re0 + re1, re0 - re1, axis), join(im0 + im1, im0 - im1, axis)))
    return outs


def forward(fields, tables):
    return forward_axis(forward_axis(fields, tables, 1), tables, 0)


def inverse(fields, tables):
    return inverse_axis(inverse_axis(fields, tables, 0), tables, 1)


def times(left, right):
    return (left[0] * right[0] - left[1] * right[1], left[0] * right[1] + left[1] * right[0])


def conj_times(left, right):
    return (left[0] * right[0] + left[1] * right[1], left[0] * right[1] - left[1] * right[0])


def cut_lanes(strip, shift):
    turned = [pltpu.roll(strip[:, k * HALF:(k + 1) * HALF], (HALF - shift) & (HALF - 1), 1) for k in range(3)]
    kept = lax.broadcasted_iota(jnp.int32, turned[0].shape, 1) < HALF - shift
    return jnp.concatenate([jnp.where(kept, turned[k], turned[k + 1]) for k in range(2)], axis=1)


def put_lanes(value, shift):
    turned = [pltpu.roll(value[:, k * HALF:(k + 1) * HALF], shift, 1) for k in range(2)]
    kept = lax.broadcasted_iota(jnp.int32, turned[0].shape, 1) >= shift
    return jnp.concatenate(
        [jnp.where(kept, turned[0], 0.0), jnp.where(kept, turned[1], turned[0]), jnp.where(kept, 0.0, turned[1])],
        axis=1,
    )


def cut_rows(strip, shift):
    groups = pltpu.roll(strip.reshape(WIN // 8 + 1, 8, strip.shape[1]), (8 - shift) & 7, 1)
    kept = lax.broadcasted_iota(jnp.int32, (WIN // 8, 8, strip.shape[1]), 1) < 8 - shift
    return jnp.where(kept, groups[:-1], groups[1:]).reshape(WIN, strip.shape[1])


def put_rows(value, shift):
    groups = pltpu.roll(value.reshape(WIN // 8, 8, value.shape[1]), shift, 1)
    none = jnp.zeros((1, 8, value.shape[1]), F32)
    kept = lax.broadcasted_iota(jnp.int32, (WIN // 8 + 1, 8, value.shape[1]), 1) >= shift
    here = jnp.concatenate([groups, none], axis=0)
    before = jnp.concatenate([none, groups], axis=0)
    return jnp.where(kept, here, before).reshape(WIN + 8, value.shape[1])


def pieces(place, field, middle, sibling, other):
    tops = (HALF, pl.multiple_of(place[4], HALF), pl.multiple_of(place[5], HALF))
    for k in range(3):
        rows = pl.ds(tops[k], HALF)
        yield middle[k], field.at[:, rows, HALF:2 * HALF]
        yield sibling[k], field.at[:, rows, pl.ds(pl.multiple_of(place[6], HALF), HALF)]
        yield other[k], field.at[:, rows, pl.ds(pl.multiple_of(place[7], HALF), HALF)]


def spot(place, slot):
    row, col = (place[2 * slot], place[2 * slot + 1])
    low = row % 8
    return pl.multiple_of(row - low, 8), low, col


def window(field, place, slot):
    base, low, col = spot(place, slot)
    strips = [field[part, pl.ds(base, WIN + 8), :] for part in range(2)]
    return tuple(cut_rows(cut_lanes(strip, col), low) for strip in strips)


def add_window(field, place, slot, term):
    base, low, col = spot(place, slot)
    for part in range(2):
        field[part, pl.ds(base, WIN + 8), :] += put_lanes(put_rows(term[part], low), col)


def assemble(place, field, layer, own, near, far, sibling, other, arrived):
    middle = [tile.at[layer] for tile in (own, near, far)]
    parts = pieces(place, field, middle, [sibling.at[k] for k in range(3)], [other.at[k] for k in range(3)])
    return [pltpu.make_async_copy(a, b, arrived.at[n]) for n, (a, b) in enumerate(parts)]


def front_kernel(place, own, near, far, sibling, other, probe, propagator, tables, out_wave, out_layer, field, arrived):
    loads = assemble(place, field, 0, own, near, far, sibling, other, arrived)
    for load in loads:
        load.start()
    wave = (probe[0].astype(F32), probe[1].astype(F32))
    spread = (propagator[0], propagator[1])
    for load in loads:
        load.wait()
    layers = [window(field, place, slot) for slot in range(2)]
    spectra = forward([times(wave, layer) for layer in layers], tables)
    entering = inverse([times(spectrum, spread) for spectrum in spectra], tables)
    for slot in range(2):
        for part in range(2):
            out_layer[slot, part] = layers[slot][part]
            out_wave[slot, part] = entering[slot][part]


def back_kernel(place, weight, own, near, far, sibling, other, waves, layers, probe, propagator, intensity, tables,
                out_own, out_near, out_far, out_sibling, out_other, out_probe, field, total0, total1, kept, arrived, left_sem):
    loads = assemble(place, field, 1, own, near, far, sibling, other, arrived)
    for load in loads:
        load.start()
    totals = (total0, total1)

    def stores(layer):
        middle = [tile.at[layer] for tile in (out_own, out_near, out_far)]
        sides = [[side.at[k, layer] for k in range(3)] for side in (out_sibling, out_other)]
        parts = pieces(place, totals[layer], middle, *sides)
        return [pltpu.make_async_copy(b, a, left_sem.at[layer, n]) for n, (a, b) in enumerate(parts)]

    for total in totals:
        total[...] = jnp.zeros(total.shape, F32)
    spread = (propagator[0], propagator[1])
    for load in loads:
        load.wait()
    two = range(2)
    spectra = forward([times((waves[slot, 0], waves[slot, 1]), window(field, place, slot)) for slot in two], tables)
    fields = []
    for slot in two:
        spectrum = spectra[slot]
        power = spectrum[0] * spectrum[0] + spectrum[1] * spectrum[1]
        misfit = weight[slot] * (power - intensity[slot])
        fields.append((misfit * spectrum[0], misfit * spectrum[1]))
    adjoint = inverse(fields, tables)
    for slot in two:
        add_window(total1, place, slot, conj_times((waves[slot, 0], waves[slot, 1]), adjoint[slot]))
        upstream = conj_times(window(field, place, slot), adjoint[slot])
        for part in range(2):
            kept[slot, part] = upstream[part]
    for store in stores(1):
        store.start()
    wave = (probe[0].astype(F32), probe[1].astype(F32))
    spectra = forward([(kept[slot, 0], kept[slot, 1]) for slot in two], tables)
    adjoint = inverse([conj_times(spread, spectrum) for spectrum in spectra], tables)
    for slot in two:
        add_window(total0, place, slot, conj_times(wave, adjoint[slot]))
    for store in stores(0):
        store.start()
    upstream = [conj_times((layers[slot, 0], layers[slot, 1]), adjoint[slot]) for slot in two]
    blocks = out_probe.shape[0]
    for part in range(2):
        out_probe[:, part] = (upstream[0][part] + upstream[1][part]).reshape(blocks, WIN // blocks, WIN)
    for layer in range(2):
        for store in stores(layer):
            store.wait()


VMEM = pl.BlockSpec(memory_space=pltpu.VMEM)
SMEM = pl.BlockSpec(memory_space=pltpu.SMEM)
ANYWHERE = pl.BlockSpec(memory_space=pl.ANY)


def shaped(*shape):
    return jax.ShapeDtypeStruct(shape, F32)


def call(kernel, out_shape, in_specs, out_specs, scratch_shapes, flops):
    return pl.pallas_call(
        kernel,
        out_shape=out_shape,
        in_specs=in_specs,
        out_specs=out_specs,
        scratch_shapes=scratch_shapes,
        compiler_params=pltpu.CompilerParams(vmem_limit_bytes=24 * 1024 * 1024),
        cost_estimate=pl.CostEstimate(flops=flops, bytes_accessed=4_000_000, transcendentals=0),
    )


def hold_kernel(stored, out, arrived):
    load = pltpu.make_async_copy(stored, out, arrived)
    load.start()
    load.wait()


def hold(tables):
    return call(
        hold_kernel,
        jax.ShapeDtypeStruct(tables.shape, BF16),
        [ANYWHERE],
        VMEM,
        [pltpu.SemaphoreType.DMA],
        0,
    )(tables)


def front(place, tiles, probe, propagator, tables):
    return call(
        front_kernel,
        [shaped(2, 2, WIN, WIN)] * 2,
        [SMEM] + [ANYWHERE] * 5 + [VMEM] * 3,
        [VMEM] * 2,
        [pltpu.VMEM((2, 3 * HALF, 3 * HALF), F32), pltpu.SemaphoreType.DMA((9,))],
        3_300_000_000,
    )(place, *tiles, probe, propagator, tables)


def back(place, weight, tiles, waves, layers, probe, propagator, intensity, tables, blocks):
    return call(
        back_kernel,
        [shaped(2, 2, HALF, HALF)] * 3 + [shaped(3, 2, 2, HALF, HALF)] * 2 + [shaped(blocks, 2, WIN // blocks, WIN)],
        [SMEM] * 2 + [ANYWHERE] * 5 + [VMEM] * 6,
        [ANYWHERE] * 5 + [VMEM],
        [pltpu.VMEM((2, 3 * HALF, 3 * HALF), F32)] * 3
        + [pltpu.VMEM((2, 2, WIN, WIN), F32), pltpu.SemaphoreType.DMA((9,)), pltpu.SemaphoreType.DMA((2, 9))],
        6_600_000_000,
    )(place, weight, *tiles, waves, layers, probe, propagator, intensity, tables)


def flipped(pairs):
    return [(j, i) for i, j in pairs]


def sides(value):
    cols = lax.axis_size("col")
    inner = [(i, i + 1) for i in range(1, cols - 1, 2)]
    other = lax.ppermute(value, "col", inner + flipped(inner))
    return lax.ppermute(value, "col", [(i, i ^ 1) for i in range(cols)]), other


def probe_rows(term):
    rows = lax.axis_size("row")
    groups = [[2 * k + half for k in range(rows // 2)] for half in range(2)]
    return lax.all_to_all(term, "row", 0, 0, tiled=True, axis_index_groups=groups)


def probe_block(pair, own):
    rows, cols = (lax.axis_size("row"), lax.axis_size("col"))
    size, width = (WIN // rows, WIN // cols)
    parts = pair.reshape(2, 2, size, cols, width).transpose(1, 3, 0, 2, 4).reshape(2 * cols, 2, size * width)
    groups = [[(2 * k + half) * cols + c for half in range(2) for c in range(cols)] for k in range(rows // 2)]
    gathered = lax.all_to_all(parts, ("row", "col"), 0, 0, tiled=True, axis_index_groups=groups)
    own, gathered = lax.optimization_barrier((own, gathered))
    return own, jnp.sum(gathered, axis=0).reshape(2, size, width)


def per_device(object_slices, probe_wave, propagator_phase, intensity, centres, batch_order):
    rows = lax.axis_size("row")
    row, col = (lax.axis_index("row"), lax.axis_index("col"))
    hops = [(i, i + 2) for i in range(0, rows - 2, 2)] + [(i + 2, i) for i in range(1, rows - 2, 2)]
    swap = [(i, i ^ 1) for i in range(rows)]
    near = lax.ppermute(object_slices, "row", swap)
    order = order_matrix()
    angles = dot(dot(order, propagator_phase).astype(BF16), order.T)
    propagator = jnp.stack([jnp.cos(angles), jnp.sin(angles)])
    middle = jnp.einsum("ab,sbc->sac", order, intensity[0, 0], preferred_element_type=F32).astype(BF16)
    measured = jnp.einsum("sac,dc->sad", middle, order, preferred_element_type=F32)
    upper, odd = (row % 2, col % 2)
    place = jnp.concatenate([
        (centres[0, 0] - jnp.stack([row * HALF, col * HALF])).reshape(4),
        2 * HALF * jnp.stack([1 - upper, upper, 1 - odd, odd]),
    ]).astype(jnp.int32)
    weight = (batch_order[0, 0] >= 0).astype(F32)
    tables = hold(half_tables())
    ready = (near, propagator, measured, place, weight, tables)
    near, propagator, measured, place, weight, tables = lax.optimization_barrier(ready)
    far = lax.ppermute(near, "row", hops)
    tiles = (object_slices, near, far)
    stacks = lax.optimization_barrier([jnp.stack([object_slices[k], near[k], near[k]]) for k in range(2)])
    sent = [lax.dynamic_update_slice(stacks[k], far[k][None], (2, 0, 0, 0)) for k in range(2)]
    sides0, sides1 = (sides(sent[0]), sides(sent[1]))

    waves, layers = front(place, tiles + sides0, probe_wave, propagator, tables)
    outs = back(place, weight, tiles + sides1, waves, layers, probe_wave, propagator, measured, tables, rows // 2)
    own, near, far, to_sibling, to_other, probe_term = outs
    cols = lax.axis_size("col")
    inner = [(i, i + 1) for i in range(1, cols - 1, 2)]
    other = lax.ppermute(to_other, "col", inner + flipped(inner))
    sibling = lax.ppermute(to_sibling, "col", [(i, i ^ 1) for i in range(cols)])
    spread = probe_rows(probe_term)
    far = lax.ppermute(far + sibling[2] + other[2], "row", flipped(hops))
    pair = jnp.sum(spread, axis=0)
    near = near + sibling[1] + other[1] + far
    own = own + sibling[0] + other[0] + lax.ppermute(near, "row", swap)
    return probe_block(pair, own)


def solution(mesh):
    placed = (
        P(None, None, "row", "col"),
        P(),
        P(),
        P("row", "col", None, None, None),
        P("row", "col", None, None),
        P("row", "col", None),
    )
    return jax.shard_map(
        per_device,
        mesh=mesh,
        in_specs=placed,
        out_specs=(P(None, None, "row", "col"), P(None, "row", "col")),
        check_vma=False,
    )
```

```python
import math

import jax
import jax.numpy as jnp
import numpy as np
from jax import lax
from jax.experimental import pallas as pl
from jax.experimental.pallas import tpu as pltpu
from jax.sharding import PartitionSpec as P

WIN = 256
HALF = 128
F32 = jnp.float32
BF16 = jnp.bfloat16


def frequency_order():
    return np.concatenate([np.arange(0, WIN, 2), np.arange(1, WIN, 2)])


def order_matrix():
    matrix = np.zeros((WIN, WIN), np.float32)
    matrix[np.arange(WIN), frequency_order()] = 1.0
    return jnp.asarray(matrix, BF16)


def half_tables():
    spots = np.arange(HALF)
    tables = []
    for parity in range(2):
        angles = 2.0 * math.pi * (np.outer(spots, 2 * spots + parity) % WIN) / WIN
        cosine, sine = (np.cos(angles) / 16.0, np.sin(angles) / 16.0)
        block = np.block([[cosine, -sine], [sine, cosine]])
        tables += [block, block.T]
    exact = np.stack(tables).astype(np.float32)
    high = exact.astype(jnp.bfloat16)
    low = (exact - high.astype(np.float32)).astype(jnp.bfloat16)
    return jnp.asarray(np.stack([high, low], axis=1))


def split(value):
    high = value.astype(BF16)
    return high, (value - high.astype(F32)).astype(BF16)


def dot(left, right):
    return jnp.dot(left, right, preferred_element_type=F32)


def right_mul(value, table_ref, index):
    high, low = split(value)
    table = table_ref[index, 0]
    both = dot(join(high, low, 0), table)
    size = value.shape[0]
    return both[:size] + (both[size:] + dot(high, table_ref[index, 1]))


def left_mul(table_ref, index, value):
    high, low = split(value)
    table = table_ref[index, 0]
    both = dot(join(table, table_ref[index, 1], 0), high)
    size = table.shape[0]
    return both[:size] + (dot(table, low) + both[size:])


def join(first, second, axis):
    return jnp.concatenate([first, second], axis=axis)


def halves(value, axis):
    if axis == 0:
        return value[:HALF], value[HALF:]
    return value[:, :HALF], value[:, HALF:]


def mul_all(values, tables, index, axis):
    if axis == 1:
        out = right_mul(jnp.concatenate(values, axis=0), tables, index)
        return [out[n * WIN:(n + 1) * WIN] for n in range(len(values))]
    return [left_mul(tables, index, value) for value in values]


def forward_axis(fields, tables, axis):
    evens, odds = ([], [])
    for field in fields:
        (re0, re1), (im0, im1) = (halves(field[0], axis), halves(field[1], axis))
        evens.append(join(re0 + re1, im0 + im1, axis))
        odds.append(join(re0 - re1, im0 - im1, axis))
    evens = mul_all(evens, tables, 0 if axis == 1 else 1, axis)
    odds = mul_all(odds, tables, 2 if axis == 1 else 3, axis)
    outs = []
    for even, odd in zip(evens, odds):
        (re0, im0), (re1, im1) = (halves(even, axis), halves(odd, axis))
        outs.append((join(re0, re1, axis), join(im0, im1, axis)))
    return outs


def inverse_axis(fields, tables, axis):
    evens, odds = ([], [])
    for field in fields:
        (re0, re1), (im0, im1) = (halves(field[0], axis), halves(field[1], axis))
        evens.append(join(re0, im0, axis))
        odds.append(join(re1, im1, axis))
    evens = mul_all(evens, tables, 1 if axis == 1 else 0, axis)
    odds = mul_all(odds, tables, 3 if axis == 1 else 2, axis)
    outs = []
    for even, odd in zip(evens, odds):
        (re0, im0), (re1, im1) = (halves(even, axis), halves(odd, axis))
        outs.append((join(re0 + re1, re0 - re1, axis), join(im0 + im1, im0 - im1, axis)))
    return outs


def forward(fields, tables):
    return forward_axis(forward_axis(fields, tables, 1), tables, 0)


def inverse(fields, tables):
    return inverse_axis(inverse_axis(fields, tables, 0), tables, 1)


def times(left, right):
    return (left[0] * right[0] - left[1] * right[1], left[0] * right[1] + left[1] * right[0])


def conj_times(left, right):
    return (left[0] * right[0] + left[1] * right[1], left[0] * right[1] - left[1] * right[0])


def cut_lanes(strip, shift):
    turned = [pltpu.roll(strip[:, k * HALF:(k + 1) * HALF], (HALF - shift) & (HALF - 1), 1) for k in range(3)]
    kept = lax.broadcasted_iota(jnp.int32, turned[0].shape, 1) < HALF - shift
    return jnp.concatenate([jnp.where(kept, turned[k], turned[k + 1]) for k in range(2)], axis=1)


def put_lanes(value, shift):
    turned = [pltpu.roll(value[:, k * HALF:(k + 1) * HALF], shift, 1) for k in range(2)]
    kept = lax.broadcasted_iota(jnp.int32, turned[0].shape, 1) >= shift
    return jnp.concatenate(
        [jnp.where(kept, turned[0], 0.0), jnp.where(kept, turned[1], turned[0]), jnp.where(kept, 0.0, turned[1])],
        axis=1,
    )


def cut_rows(strip, shift):
    groups = pltpu.roll(strip.reshape(WIN // 8 + 1, 8, strip.shape[1]), (8 - shift) & 7, 1)
    kept = lax.broadcasted_iota(jnp.int32, (WIN // 8, 8, strip.shape[1]), 1) < 8 - shift
    return jnp.where(kept, groups[:-1], groups[1:]).reshape(WIN, strip.shape[1])


def put_rows(value, shift):
    groups = pltpu.roll(value.reshape(WIN // 8, 8, value.shape[1]), shift, 1)
    none = jnp.zeros((1, 8, value.shape[1]), F32)
    kept = lax.broadcasted_iota(jnp.int32, (WIN // 8 + 1, 8, value.shape[1]), 1) >= shift
    here = jnp.concatenate([groups, none], axis=0)
    before = jnp.concatenate([none, groups], axis=0)
    return jnp.where(kept, here, before).reshape(WIN + 8, value.shape[1])


def pieces(place, field, middle, sibling, other):
    tops = (HALF, pl.multiple_of(place[4], HALF), pl.multiple_of(place[5], HALF))
    for k in range(3):
        rows = pl.ds(tops[k], HALF)
        yield middle[k], field.at[:, rows, HALF:2 * HALF]
        yield sibling[k], field.at[:, rows, pl.ds(pl.multiple_of(place[6], HALF), HALF)]
        yield other[k], field.at[:, rows, pl.ds(pl.multiple_of(place[7], HALF), HALF)]


def spot(place, slot):
    row, col = (place[2 * slot], place[2 * slot + 1])
    low = row % 8
    return pl.multiple_of(row - low, 8), low, col


def window(field, place, slot):
    base, low, col = spot(place, slot)
    strips = [field[part, pl.ds(base, WIN + 8), :] for part in range(2)]
    return tuple(cut_rows(cut_lanes(strip, col), low) for strip in strips)


def add_window(field, place, slot, term):
    base, low, col = spot(place, slot)
    for part in range(2):
        field[part, pl.ds(base, WIN + 8), :] += put_lanes(put_rows(term[part], low), col)


def assemble(place, field, layer, own, near, far, sibling, other, arrived):
    middle = [tile.at[layer] for tile in (own, near, far)]
    parts = pieces(place, field, middle, [sibling.at[k] for k in range(3)], [other.at[k] for k in range(3)])
    return [pltpu.make_async_copy(a, b, arrived.at[n]) for n, (a, b) in enumerate(parts)]


def front_kernel(place, own, near, far, sibling, other, probe, propagator, tables, out_wave, out_layer, field, arrived):
    loads = assemble(place, field, 0, own, near, far, sibling, other, arrived)
    for load in loads:
        load.start()
    wave = (probe[0].astype(F32), probe[1].astype(F32))
    spread = (propagator[0], propagator[1])
    for load in loads:
        load.wait()
    layers = [window(field, place, slot) for slot in range(2)]
    spectra = forward([times(wave, layer) for layer in layers], tables)
    entering = inverse([times(spectrum, spread) for spectrum in spectra], tables)
    for slot in range(2):
        for part in range(2):
            out_layer[slot, part] = layers[slot][part]
            out_wave[slot, part] = entering[slot][part]


def back_kernel(place, weight, own, near, far, sibling, other, waves, layers, probe, propagator, intensity, tables,
                out_own, out_near, out_far, out_sibling, out_other, out_last, out_probe, field, total0, total1, kept, arrived, left_sem):
    loads = assemble(place, field, 1, own, near, far, sibling, other, arrived)
    for load in loads:
        load.start()
    totals = (total0, total1)

    def stores(layer):
        middle = [tile.at[layer] for tile in (out_own, out_near, out_far)]
        beside = [out_sibling.at[k, layer] for k in range(3)]
        beyond = [out_other.at[0, layer], out_other.at[1, layer], out_last.at[layer]]
        parts = pieces(place, totals[layer], middle, beside, beyond)
        return [pltpu.make_async_copy(b, a, left_sem.at[layer, n]) for n, (a, b) in enumerate(parts)]

    for total in totals:
        total[...] = jnp.zeros(total.shape, F32)
    spread = (propagator[0], propagator[1])
    for load in loads:
        load.wait()
    two = range(2)
    spectra = forward([times((waves[slot, 0], waves[slot, 1]), window(field, place, slot)) for slot in two], tables)
    fields = []
    for slot in two:
        spectrum = spectra[slot]
        power = spectrum[0] * spectrum[0] + spectrum[1] * spectrum[1]
        misfit = weight[slot] * (power - intensity[slot])
        fields.append((misfit * spectrum[0], misfit * spectrum[1]))
    adjoint = inverse(fields, tables)
    for slot in two:
        add_window(total1, place, slot, conj_times((waves[slot, 0], waves[slot, 1]), adjoint[slot]))
        upstream = conj_times(window(field, place, slot), adjoint[slot])
        for part in range(2):
            kept[slot, part] = upstream[part]
    for store in stores(1):
        store.start()
    wave = (probe[0].astype(F32), probe[1].astype(F32))
    spectra = forward([(kept[slot, 0], kept[slot, 1]) for slot in two], tables)
    adjoint = inverse([conj_times(spread, spectrum) for spectrum in spectra], tables)
    for slot in two:
        add_window(total0, place, slot, conj_times(wave, adjoint[slot]))
    for store in stores(0):
        store.start()
    upstream = [conj_times((layers[slot, 0], layers[slot, 1]), adjoint[slot]) for slot in two]
    blocks = out_probe.shape[0]
    for part in range(2):
        out_probe[:, part] = (upstream[0][part] + upstream[1][part]).reshape(blocks, WIN // blocks, WIN)
    for layer in range(2):
        for store in stores(layer):
            store.wait()


VMEM = pl.BlockSpec(memory_space=pltpu.VMEM)
SMEM = pl.BlockSpec(memory_space=pltpu.SMEM)
ANYWHERE = pl.BlockSpec(memory_space=pl.ANY)


def shaped(*shape):
    return jax.ShapeDtypeStruct(shape, F32)


def call(kernel, out_shape, in_specs, out_specs, scratch_shapes, flops):
    return pl.pallas_call(
        kernel,
        out_shape=out_shape,
        in_specs=in_specs,
        out_specs=out_specs,
        scratch_shapes=scratch_shapes,
        compiler_params=pltpu.CompilerParams(vmem_limit_bytes=24 * 1024 * 1024),
        cost_estimate=pl.CostEstimate(flops=flops, bytes_accessed=4_000_000, transcendentals=0),
    )


def hold_kernel(stored, out, arrived):
    load = pltpu.make_async_copy(stored, out, arrived)
    load.start()
    load.wait()


def hold(tables):
    return call(
        hold_kernel,
        jax.ShapeDtypeStruct(tables.shape, BF16),
        [ANYWHERE],
        VMEM,
        [pltpu.SemaphoreType.DMA],
        0,
    )(tables)


def front(place, tiles, probe, propagator, tables):
    return call(
        front_kernel,
        [shaped(2, 2, WIN, WIN)] * 2,
        [SMEM] + [ANYWHERE] * 5 + [VMEM] * 3,
        [VMEM] * 2,
        [pltpu.VMEM((2, 3 * HALF, 3 * HALF), F32), pltpu.SemaphoreType.DMA((9,))],
        3_300_000_000,
    )(place, *tiles, probe, propagator, tables)


def back(place, weight, tiles, waves, layers, probe, propagator, intensity, tables, blocks):
    return call(
        back_kernel,
        [shaped(2, 2, HALF, HALF)] * 3
        + [shaped(3, 2, 2, HALF, HALF), shaped(2, 2, 2, HALF, HALF), shaped(2, 2, HALF, HALF)]
        + [shaped(blocks, 2, WIN // blocks, WIN)],
        [SMEM] * 2 + [ANYWHERE] * 5 + [VMEM] * 6,
        [ANYWHERE] * 6 + [VMEM],
        [pltpu.VMEM((2, 3 * HALF, 3 * HALF), F32)] * 3
        + [pltpu.VMEM((2, 2, WIN, WIN), F32), pltpu.SemaphoreType.DMA((9,)), pltpu.SemaphoreType.DMA((2, 9))],
        6_600_000_000,
    )(place, weight, *tiles, waves, layers, probe, propagator, intensity, tables)


def flipped(pairs):
    return [(j, i) for i, j in pairs]


def sides(value):
    cols = lax.axis_size("col")
    inner = [(i, i + 1) for i in range(1, cols - 1, 2)]
    other = lax.ppermute(value, "col", inner + flipped(inner))
    return lax.ppermute(value, "col", [(i, i ^ 1) for i in range(cols)]), other


def probe_rows(term):
    rows = lax.axis_size("row")
    groups = [[2 * k + half for k in range(rows // 2)] for half in range(2)]
    return lax.all_to_all(term, "row", 0, 0, tiled=True, axis_index_groups=groups)


def probe_block(pair, own):
    rows, cols = (lax.axis_size("row"), lax.axis_size("col"))
    size, width = (WIN // rows, WIN // cols)
    parts = pair.reshape(2, 2, size, cols, width).transpose(1, 3, 0, 2, 4).reshape(2 * cols, 2, size * width)
    groups = [[(2 * k + half) * cols + c for half in range(2) for c in range(cols)] for k in range(rows // 2)]
    gathered = lax.all_to_all(parts, ("row", "col"), 0, 0, tiled=True, axis_index_groups=groups)
    own, gathered = lax.optimization_barrier((own, gathered))
    return own, jnp.sum(gathered, axis=0).reshape(2, size, width)


def per_device(object_slices, probe_wave, propagator_phase, intensity, centres, batch_order):
    rows = lax.axis_size("row")
    row, col = (lax.axis_index("row"), lax.axis_index("col"))
    hops = [(i, i + 2) for i in range(0, rows - 2, 2)] + [(i + 2, i) for i in range(1, rows - 2, 2)]
    swap = [(i, i ^ 1) for i in range(rows)]
    near = lax.ppermute(object_slices, "row", swap)
    order = order_matrix()
    angles = dot(dot(order, propagator_phase).astype(BF16), order.T)
    propagator = jnp.stack([jnp.cos(angles), jnp.sin(angles)])
    middle = jnp.einsum("ab,sbc->sac", order, intensity[0, 0], preferred_element_type=F32).astype(BF16)
    measured = jnp.einsum("sac,dc->sad", middle, order, preferred_element_type=F32)
    upper, odd = (row % 2, col % 2)
    place = jnp.concatenate([
        (centres[0, 0] - jnp.stack([row * HALF, col * HALF])).reshape(4),
        2 * HALF * jnp.stack([1 - upper, upper, 1 - odd, odd]),
    ]).astype(jnp.int32)
    weight = (batch_order[0, 0] >= 0).astype(F32)
    tables = hold(half_tables())
    ready = (near, propagator, measured, place, weight, tables)
    near, propagator, measured, place, weight, tables = lax.optimization_barrier(ready)
    far = lax.ppermute(near, "row", hops)
    tiles = (object_slices, near, far)
    stacks = lax.optimization_barrier([jnp.stack([object_slices[k], near[k], near[k]]) for k in range(2)])
    sent = [lax.dynamic_update_slice(stacks[k], far[k][None], (2, 0, 0, 0)) for k in range(2)]
    sides0, sides1 = (sides(sent[0]), sides(sent[1]))

    waves, layers = front(place, tiles + sides0, probe_wave, propagator, tables)
    outs = back(place, weight, tiles + sides1, waves, layers, probe_wave, propagator, measured, tables, rows // 2)
    own, near, far, to_sibling, to_other, to_last, probe_term = outs
    cols = lax.axis_size("col")
    inner = [(i, i + 1) for i in range(1, cols - 1, 2)]
    last = lax.ppermute(to_last, "col", inner + flipped(inner))
    other = lax.ppermute(to_other, "col", inner + flipped(inner))
    sibling = lax.ppermute(to_sibling, "col", [(i, i ^ 1) for i in range(cols)])
    spread = probe_rows(probe_term)
    far = lax.ppermute(far + sibling[2] + last, "row", flipped(hops))
    pair = jnp.sum(spread, axis=0)
    near = near + sibling[1] + other[1] + far
    own = own + sibling[0] + other[0] + lax.ppermute(near, "row", swap)
    return probe_block(pair, own)


def solution(mesh):
    placed = (
        P(None, None, "row", "col"),
        P(),
        P(),
        P("row", "col", None, None, None),
        P("row", "col", None, None),
        P("row", "col", None),
    )
    return jax.shard_map(
        per_device,
        mesh=mesh,
        in_specs=placed,
        out_specs=(P(None, None, "row", "col"), P(None, "row", "col")),
        check_vma=False,
    )
```

```python
import math

import jax
import jax.numpy as jnp
import numpy as np
from jax import lax
from jax.experimental import pallas as pl
from jax.experimental.pallas import tpu as pltpu
from jax.sharding import PartitionSpec as P

WIN = 256
HALF = 128
F32 = jnp.float32
BF16 = jnp.bfloat16


def frequency_order():
    return np.concatenate([np.arange(0, WIN, 2), np.arange(1, WIN, 2)])


def order_matrix():
    matrix = np.zeros((WIN, WIN), np.float32)
    matrix[np.arange(WIN), frequency_order()] = 1.0
    return jnp.asarray(matrix, BF16)


def half_tables():
    spots = np.arange(HALF)
    tables = []
    for parity in range(2):
        angles = 2.0 * math.pi * (np.outer(spots, 2 * spots + parity) % WIN) / WIN
        cosine, sine = (np.cos(angles) / 16.0, np.sin(angles) / 16.0)
        block = np.block([[cosine, -sine], [sine, cosine]])
        tables += [block, block.T]
    exact = np.stack(tables).astype(np.float32)
    high = exact.astype(jnp.bfloat16)
    low = (exact - high.astype(np.float32)).astype(jnp.bfloat16)
    return jnp.asarray(np.stack([high, low], axis=1))


def split(value):
    high = value.astype(BF16)
    return high, (value - high.astype(F32)).astype(BF16)


def dot(left, right):
    return jnp.dot(left, right, preferred_element_type=F32)


def right_mul(value, table_ref, index):
    high, low = split(value)
    table = table_ref[index, 0]
    both = dot(join(high, low, 0), table)
    size = value.shape[0]
    return both[:size] + (both[size:] + dot(high, table_ref[index, 1]))


def left_mul(table_ref, index, value):
    high, low = split(value)
    table = table_ref[index, 0]
    both = dot(join(table, table_ref[index, 1], 0), high)
    size = table.shape[0]
    return both[:size] + (dot(table, low) + both[size:])


def join(first, second, axis):
    return jnp.concatenate([first, second], axis=axis)


def halves(value, axis):
    if axis == 0:
        return value[:HALF], value[HALF:]
    return value[:, :HALF], value[:, HALF:]


def mul_all(values, tables, index, axis):
    if axis == 1:
        out = right_mul(jnp.concatenate(values, axis=0), tables, index)
        return [out[n * WIN:(n + 1) * WIN] for n in range(len(values))]
    out = left_mul(tables, index, jnp.concatenate(values, axis=1))
    return [out[:, n * WIN:(n + 1) * WIN] for n in range(len(values))]


def forward_axis(fields, tables, axis):
    evens, odds = ([], [])
    for field in fields:
        (re0, re1), (im0, im1) = (halves(field[0], axis), halves(field[1], axis))
        evens.append(join(re0 + re1, im0 + im1, axis))
        odds.append(join(re0 - re1, im0 - im1, axis))
    evens = mul_all(evens, tables, 0 if axis == 1 else 1, axis)
    odds = mul_all(odds, tables, 2 if axis == 1 else 3, axis)
    outs = []
    for even, odd in zip(evens, odds):
        (re0, im0), (re1, im1) = (halves(even, axis), halves(odd, axis))
        outs.append((join(re0, re1, axis), join(im0, im1, axis)))
    return outs


def inverse_axis(fields, tables, axis):
    evens, odds = ([], [])
    for field in fields:
        (re0, re1), (im0, im1) = (halves(field[0], axis), halves(field[1], axis))
        evens.append(join(re0, im0, axis))
        odds.append(join(re1, im1, axis))
    evens = mul_all(evens, tables, 1 if axis == 1 else 0, axis)
    odds = mul_all(odds, tables, 3 if axis == 1 else 2, axis)
    outs = []
    for even, odd in zip(evens, odds):
        (re0, im0), (re1, im1) = (halves(even, axis), halves(odd, axis))
        outs.append((join(re0 + re1, re0 - re1, axis), join(im0 + im1, im0 - im1, axis)))
    return outs


def forward(fields, tables):
    return forward_axis(forward_axis(fields, tables, 1), tables, 0)


def inverse(fields, tables):
    return inverse_axis(inverse_axis(fields, tables, 0), tables, 1)


def times(left, right):
    return (left[0] * right[0] - left[1] * right[1], left[0] * right[1] + left[1] * right[0])


def conj_times(left, right):
    return (left[0] * right[0] + left[1] * right[1], left[0] * right[1] - left[1] * right[0])


def cut_lanes(strip, shift):
    turned = [pltpu.roll(strip[:, k * HALF:(k + 1) * HALF], (HALF - shift) & (HALF - 1), 1) for k in range(3)]
    kept = lax.broadcasted_iota(jnp.int32, turned[0].shape, 1) < HALF - shift
    return jnp.concatenate([jnp.where(kept, turned[k], turned[k + 1]) for k in range(2)], axis=1)


def put_lanes(value, shift):
    turned = [pltpu.roll(value[:, k * HALF:(k + 1) * HALF], shift, 1) for k in range(2)]
    kept = lax.broadcasted_iota(jnp.int32, turned[0].shape, 1) >= shift
    return jnp.concatenate(
        [jnp.where(kept, turned[0], 0.0), jnp.where(kept, turned[1], turned[0]), jnp.where(kept, 0.0, turned[1])],
        axis=1,
    )


def cut_rows(strip, shift):
    groups = pltpu.roll(strip.reshape(WIN // 8 + 1, 8, strip.shape[1]), (8 - shift) & 7, 1)
    kept = lax.broadcasted_iota(jnp.int32, (WIN // 8, 8, strip.shape[1]), 1) < 8 - shift
    return jnp.where(kept, groups[:-1], groups[1:]).reshape(WIN, strip.shape[1])


def put_rows(value, shift):
    groups = pltpu.roll(value.reshape(WIN // 8, 8, value.shape[1]), shift, 1)
    none = jnp.zeros((1, 8, value.shape[1]), F32)
    kept = lax.broadcasted_iota(jnp.int32, (WIN // 8 + 1, 8, value.shape[1]), 1) >= shift
    here = jnp.concatenate([groups, none], axis=0)
    before = jnp.concatenate([none, groups], axis=0)
    return jnp.where(kept, here, before).reshape(WIN + 8, value.shape[1])


def pieces(place, field, middle, sibling, other):
    tops = (HALF, pl.multiple_of(place[4], HALF), pl.multiple_of(place[5], HALF))
    for k in range(3):
        rows = pl.ds(tops[k], HALF)
        yield middle[k], field.at[:, rows, HALF:2 * HALF]
        yield sibling[k], field.at[:, rows, pl.ds(pl.multiple_of(place[6], HALF), HALF)]
        yield other[k], field.at[:, rows, pl.ds(pl.multiple_of(place[7], HALF), HALF)]


def spot(place, slot):
    row, col = (place[2 * slot], place[2 * slot + 1])
    low = row % 8
    return pl.multiple_of(row - low, 8), low, col


def window(field, place, slot):
    base, low, col = spot(place, slot)
    strips = [field[part, pl.ds(base, WIN + 8), :] for part in range(2)]
    return tuple(cut_rows(cut_lanes(strip, col), low) for strip in strips)


def add_window(field, place, slot, term):
    base, low, col = spot(place, slot)
    for part in range(2):
        field[part, pl.ds(base, WIN + 8), :] += put_lanes(put_rows(term[part], low), col)


def assemble(place, field, layer, own, near, far, sibling, other, arrived):
    middle = [tile.at[layer] for tile in (own, near, far)]
    parts = pieces(place, field, middle, [sibling.at[k] for k in range(3)], [other.at[k] for k in range(3)])
    return [pltpu.make_async_copy(a, b, arrived.at[n]) for n, (a, b) in enumerate(parts)]


def front_kernel(place, own, near, far, sibling, other, probe, propagator, tables, out_wave, out_layer, field, arrived):
    loads = assemble(place, field, 0, own, near, far, sibling, other, arrived)
    for load in loads:
        load.start()
    wave = (probe[0].astype(F32), probe[1].astype(F32))
    spread = (propagator[0], propagator[1])
    for load in loads:
        load.wait()
    layers = [window(field, place, slot) for slot in range(2)]
    spectra = forward([times(wave, layer) for layer in layers], tables)
    entering = inverse([times(spectrum, spread) for spectrum in spectra], tables)
    for slot in range(2):
        for part in range(2):
            out_layer[slot, part] = layers[slot][part]
            out_wave[slot, part] = entering[slot][part]


def back_kernel(place, weight, own, near, far, sibling, other, waves, layers, probe, propagator, intensity, tables,
                out_own, out_near, out_far, out_sibling, out_other, out_last, out_probe, field, total0, total1, kept, arrived, left_sem):
    loads = assemble(place, field, 1, own, near, far, sibling, other, arrived)
    for load in loads:
        load.start()
    totals = (total0, total1)

    def stores(layer):
        middle = [tile.at[layer] for tile in (out_own, out_near, out_far)]
        beside = [out_sibling.at[k, layer] for k in range(3)]
        beyond = [out_other.at[0, layer], out_other.at[1, layer], out_last.at[layer]]
        parts = pieces(place, totals[layer], middle, beside, beyond)
        return [pltpu.make_async_copy(b, a, left_sem.at[layer, n]) for n, (a, b) in enumerate(parts)]

    for total in totals:
        total[...] = jnp.zeros(total.shape, F32)
    spread = (propagator[0], propagator[1])
    for load in loads:
        load.wait()
    two = range(2)
    spectra = forward([times((waves[slot, 0], waves[slot, 1]), window(field, place, slot)) for slot in two], tables)
    fields = []
    for slot in two:
        spectrum = spectra[slot]
        power = spectrum[0] * spectrum[0] + spectrum[1] * spectrum[1]
        misfit = weight[slot] * (power - intensity[slot])
        fields.append((misfit * spectrum[0], misfit * spectrum[1]))
    adjoint = inverse(fields, tables)
    for slot in two:
        add_window(total1, place, slot, conj_times((waves[slot, 0], waves[slot, 1]), adjoint[slot]))
        upstream = conj_times(window(field, place, slot), adjoint[slot])
        for part in range(2):
            kept[slot, part] = upstream[part]
    for store in stores(1):
        store.start()
    wave = (probe[0].astype(F32), probe[1].astype(F32))
    spectra = forward([(kept[slot, 0], kept[slot, 1]) for slot in two], tables)
    adjoint = inverse([conj_times(spread, spectrum) for spectrum in spectra], tables)
    for slot in two:
        add_window(total0, place, slot, conj_times(wave, adjoint[slot]))
    for store in stores(0):
        store.start()
    upstream = [conj_times((layers[slot, 0], layers[slot, 1]), adjoint[slot]) for slot in two]
    blocks = out_probe.shape[0]
    for part in range(2):
        out_probe[:, part] = (upstream[0][part] + upstream[1][part]).reshape(blocks, WIN // blocks, WIN)
    for layer in range(2):
        for store in stores(layer):
            store.wait()


VMEM = pl.BlockSpec(memory_space=pltpu.VMEM)
SMEM = pl.BlockSpec(memory_space=pltpu.SMEM)
ANYWHERE = pl.BlockSpec(memory_space=pl.ANY)


def shaped(*shape):
    return jax.ShapeDtypeStruct(shape, F32)


def call(kernel, out_shape, in_specs, out_specs, scratch_shapes, flops):
    return pl.pallas_call(
        kernel,
        out_shape=out_shape,
        in_specs=in_specs,
        out_specs=out_specs,
        scratch_shapes=scratch_shapes,
        compiler_params=pltpu.CompilerParams(vmem_limit_bytes=24 * 1024 * 1024),
        cost_estimate=pl.CostEstimate(flops=flops, bytes_accessed=4_000_000, transcendentals=0),
    )


def hold_kernel(stored, out, arrived):
    load = pltpu.make_async_copy(stored, out, arrived)
    load.start()
    load.wait()


def hold(tables):
    return call(
        hold_kernel,
        jax.ShapeDtypeStruct(tables.shape, BF16),
        [ANYWHERE],
        VMEM,
        [pltpu.SemaphoreType.DMA],
        0,
    )(tables)


def front(place, tiles, probe, propagator, tables):
    return call(
        front_kernel,
        [shaped(2, 2, WIN, WIN)] * 2,
        [SMEM] + [ANYWHERE] * 5 + [VMEM] * 3,
        [VMEM] * 2,
        [pltpu.VMEM((2, 3 * HALF, 3 * HALF), F32), pltpu.SemaphoreType.DMA((9,))],
        3_300_000_000,
    )(place, *tiles, probe, propagator, tables)


def back(place, weight, tiles, waves, layers, probe, propagator, intensity, tables, blocks):
    return call(
        back_kernel,
        [shaped(2, 2, HALF, HALF)] * 3
        + [shaped(3, 2, 2, HALF, HALF), shaped(2, 2, 2, HALF, HALF), shaped(2, 2, HALF, HALF)]
        + [shaped(blocks, 2, WIN // blocks, WIN)],
        [SMEM] * 2 + [ANYWHERE] * 5 + [VMEM] * 6,
        [ANYWHERE] * 6 + [VMEM],
        [pltpu.VMEM((2, 3 * HALF, 3 * HALF), F32)] * 3
        + [pltpu.VMEM((2, 2, WIN, WIN), F32), pltpu.SemaphoreType.DMA((9,)), pltpu.SemaphoreType.DMA((2, 9))],
        6_600_000_000,
    )(place, weight, *tiles, waves, layers, probe, propagator, intensity, tables)


def flipped(pairs):
    return [(j, i) for i, j in pairs]


def sides(value):
    cols = lax.axis_size("col")
    inner = [(i, i + 1) for i in range(1, cols - 1, 2)]
    other = lax.ppermute(value, "col", inner + flipped(inner))
    return lax.ppermute(value, "col", [(i, i ^ 1) for i in range(cols)]), other


def probe_rows(term):
    rows = lax.axis_size("row")
    groups = [[2 * k + half for k in range(rows // 2)] for half in range(2)]
    return lax.all_to_all(term, "row", 0, 0, tiled=True, axis_index_groups=groups)


def probe_block(pair, own):
    rows, cols = (lax.axis_size("row"), lax.axis_size("col"))
    size, width = (WIN // rows, WIN // cols)
    parts = pair.reshape(2, 2, size, cols, width).transpose(1, 3, 0, 2, 4).reshape(2 * cols, 2, size * width)
    groups = [[(2 * k + half) * cols + c for half in range(2) for c in range(cols)] for k in range(rows // 2)]
    gathered = lax.all_to_all(parts, ("row", "col"), 0, 0, tiled=True, axis_index_groups=groups)
    own, gathered = lax.optimization_barrier((own, gathered))
    return own, jnp.sum(gathered, axis=0).reshape(2, size, width)


def per_device(object_slices, probe_wave, propagator_phase, intensity, centres, batch_order):
    rows = lax.axis_size("row")
    row, col = (lax.axis_index("row"), lax.axis_index("col"))
    hops = [(i, i + 2) for i in range(0, rows - 2, 2)] + [(i + 2, i) for i in range(1, rows - 2, 2)]
    swap = [(i, i ^ 1) for i in range(rows)]
    near = lax.ppermute(object_slices, "row", swap)
    order = order_matrix()
    angles = dot(dot(order, propagator_phase).astype(BF16), order.T)
    propagator = jnp.stack([jnp.cos(angles), jnp.sin(angles)])
    middle = jnp.einsum("ab,sbc->sac", order, intensity[0, 0], preferred_element_type=F32).astype(BF16)
    measured = jnp.einsum("sac,dc->sad", middle, order, preferred_element_type=F32)
    upper, odd = (row % 2, col % 2)
    place = jnp.concatenate([
        (centres[0, 0] - jnp.stack([row * HALF, col * HALF])).reshape(4),
        2 * HALF * jnp.stack([1 - upper, upper, 1 - odd, odd]),
    ]).astype(jnp.int32)
    weight = (batch_order[0, 0] >= 0).astype(F32)
    tables = hold(half_tables())
    ready = (near, propagator, measured, place, weight, tables)
    near, propagator, measured, place, weight, tables = lax.optimization_barrier(ready)
    far = lax.ppermute(near, "row", hops)
    tiles = (object_slices, near, far)
    stacks = lax.optimization_barrier([jnp.stack([object_slices[k], near[k], near[k]]) for k in range(2)])
    sent = [lax.dynamic_update_slice(stacks[k], far[k][None], (2, 0, 0, 0)) for k in range(2)]
    sides0, sides1 = (sides(sent[0]), sides(sent[1]))

    waves, layers = front(place, tiles + sides0, probe_wave, propagator, tables)
    outs = back(place, weight, tiles + sides1, waves, layers, probe_wave, propagator, measured, tables, rows // 2)
    own, near, far, to_sibling, to_other, to_last, probe_term = outs
    cols = lax.axis_size("col")
    inner = [(i, i + 1) for i in range(1, cols - 1, 2)]
    last = lax.ppermute(to_last, "col", inner + flipped(inner))
    other = lax.ppermute(to_other, "col", inner + flipped(inner))
    sibling = lax.ppermute(to_sibling, "col", [(i, i ^ 1) for i in range(cols)])
    spread = probe_rows(probe_term)
    far = lax.ppermute(far + sibling[2] + last, "row", flipped(hops))
    pair = jnp.sum(spread, axis=0)
    near = near + sibling[1] + other[1] + far
    own = own + sibling[0] + other[0] + lax.ppermute(near, "row", swap)
    return probe_block(pair, own)


def solution(mesh):
    placed = (
        P(None, None, "row", "col"),
        P(),
        P(),
        P("row", "col", None, None, None),
        P("row", "col", None, None),
        P("row", "col", None),
    )
    return jax.shard_map(
        per_device,
        mesh=mesh,
        in_specs=placed,
        out_specs=(P(None, None, "row", "col"), P(None, "row", "col")),
        check_vma=False,
    )
```

```python
import math

import jax
import jax.numpy as jnp
import numpy as np
from jax import lax
from jax.experimental import pallas as pl
from jax.experimental.pallas import tpu as pltpu
from jax.sharding import PartitionSpec as P

WIN = 256
HALF = 128
F32 = jnp.float32
BF16 = jnp.bfloat16


def frequency_order():
    return np.concatenate([np.arange(0, WIN, 2), np.arange(1, WIN, 2)])


def order_matrix():
    matrix = np.zeros((WIN, WIN), np.float32)
    matrix[np.arange(WIN), frequency_order()] = 1.0
    return jnp.asarray(matrix, BF16)


def half_tables():
    spots = np.arange(HALF)
    tables = []
    for parity in range(2):
        angles = 2.0 * math.pi * (np.outer(spots, 2 * spots + parity) % WIN) / WIN
        cosine, sine = (np.cos(angles) / 16.0, np.sin(angles) / 16.0)
        block = np.block([[cosine, -sine], [sine, cosine]])
        tables += [block, block.T]
    exact = np.stack(tables).astype(np.float32)
    high = exact.astype(jnp.bfloat16)
    low = (exact - high.astype(np.float32)).astype(jnp.bfloat16)
    return jnp.asarray(np.stack([high, low], axis=1))


def split(value):
    high = value.astype(BF16)
    return high, (value - high.astype(F32)).astype(BF16)


def dot(left, right):
    return jnp.dot(left, right, preferred_element_type=F32)


def right_mul(value, table_ref, index):
    high, low = split(value)
    table = table_ref[index, 0]
    both = dot(join(high, low, 0), table)
    size = value.shape[0]
    return both[:size] + (both[size:] + dot(high, table_ref[index, 1]))


def left_mul(table_ref, index, value):
    high, low = split(value)
    table = table_ref[index, 0]
    both = dot(join(table, table_ref[index, 1], 0), high)
    size = table.shape[0]
    return both[:size] + (dot(table, low) + both[size:])


def join(first, second, axis):
    return jnp.concatenate([first, second], axis=axis)


def halves(value, axis):
    if axis == 0:
        return value[:HALF], value[HALF:]
    return value[:, :HALF], value[:, HALF:]


def mul_all(values, tables, index, axis):
    if axis == 1:
        out = right_mul(jnp.concatenate(values, axis=0), tables, index)
        return [out[n * WIN:(n + 1) * WIN] for n in range(len(values))]
    out = left_mul(tables, index, jnp.concatenate(values, axis=1))
    return [out[:, n * WIN:(n + 1) * WIN] for n in range(len(values))]


def forward_axis(fields, tables, axis):
    evens, odds = ([], [])
    for field in fields:
        (re0, re1), (im0, im1) = (halves(field[0], axis), halves(field[1], axis))
        evens.append(join(re0 + re1, im0 + im1, axis))
        odds.append(join(re0 - re1, im0 - im1, axis))
    evens = mul_all(evens, tables, 0 if axis == 1 else 1, axis)
    odds = mul_all(odds, tables, 2 if axis == 1 else 3, axis)
    outs = []
    for even, odd in zip(evens, odds):
        (re0, im0), (re1, im1) = (halves(even, axis), halves(odd, axis))
        outs.append((join(re0, re1, axis), join(im0, im1, axis)))
    return outs


def inverse_axis(fields, tables, axis):
    evens, odds = ([], [])
    for field in fields:
        (re0, re1), (im0, im1) = (halves(field[0], axis), halves(field[1], axis))
        evens.append(join(re0, im0, axis))
        odds.append(join(re1, im1, axis))
    evens = mul_all(evens, tables, 1 if axis == 1 else 0, axis)
    odds = mul_all(odds, tables, 3 if axis == 1 else 2, axis)
    outs = []
    for even, odd in zip(evens, odds):
        (re0, im0), (re1, im1) = (halves(even, axis), halves(odd, axis))
        outs.append((join(re0 + re1, re0 - re1, axis), join(im0 + im1, im0 - im1, axis)))
    return outs


def forward(fields, tables):
    return forward_axis(forward_axis(fields, tables, 1), tables, 0)


def inverse(fields, tables):
    return inverse_axis(inverse_axis(fields, tables, 0), tables, 1)


def times(left, right):
    return (left[0] * right[0] - left[1] * right[1], left[0] * right[1] + left[1] * right[0])


def conj_times(left, right):
    return (left[0] * right[0] + left[1] * right[1], left[0] * right[1] - left[1] * right[0])


def cut_lanes(strip, shift):
    turned = [pltpu.roll(strip[:, k * HALF:(k + 1) * HALF], (HALF - shift) & (HALF - 1), 1) for k in range(3)]
    kept = lax.broadcasted_iota(jnp.int32, turned[0].shape, 1) < HALF - shift
    return jnp.concatenate([jnp.where(kept, turned[k], turned[k + 1]) for k in range(2)], axis=1)


def put_lanes(value, shift):
    turned = [pltpu.roll(value[:, k * HALF:(k + 1) * HALF], shift, 1) for k in range(2)]
    kept = lax.broadcasted_iota(jnp.int32, turned[0].shape, 1) >= shift
    return jnp.concatenate(
        [jnp.where(kept, turned[0], 0.0), jnp.where(kept, turned[1], turned[0]), jnp.where(kept, 0.0, turned[1])],
        axis=1,
    )


def cut_rows(strip, shift):
    groups = pltpu.roll(strip.reshape(WIN // 8 + 1, 8, strip.shape[1]), (8 - shift) & 7, 1)
    kept = lax.broadcasted_iota(jnp.int32, (WIN // 8, 8, strip.shape[1]), 1) < 8 - shift
    return jnp.where(kept, groups[:-1], groups[1:]).reshape(WIN, strip.shape[1])


def put_rows(value, shift):
    groups = pltpu.roll(value.reshape(WIN // 8, 8, value.shape[1]), shift, 1)
    none = jnp.zeros((1, 8, value.shape[1]), F32)
    kept = lax.broadcasted_iota(jnp.int32, (WIN // 8 + 1, 8, value.shape[1]), 1) >= shift
    here = jnp.concatenate([groups, none], axis=0)
    before = jnp.concatenate([none, groups], axis=0)
    return jnp.where(kept, here, before).reshape(WIN + 8, value.shape[1])


def pieces(place, field, middle, sibling, other):
    tops = (HALF, pl.multiple_of(place[4], HALF), pl.multiple_of(place[5], HALF))
    for k in range(3):
        rows = pl.ds(tops[k], HALF)
        yield middle[k], field.at[:, rows, HALF:2 * HALF]
        yield sibling[k], field.at[:, rows, pl.ds(pl.multiple_of(place[6], HALF), HALF)]
        yield other[k], field.at[:, rows, pl.ds(pl.multiple_of(place[7], HALF), HALF)]


def spot(place, slot):
    row, col = (place[2 * slot], place[2 * slot + 1])
    low = row % 8
    return pl.multiple_of(row - low, 8), low, col


def window(field, place, slot):
    base, low, col = spot(place, slot)
    strips = [field[part, pl.ds(base, WIN + 8), :] for part in range(2)]
    return tuple(cut_rows(cut_lanes(strip, col), low) for strip in strips)


def add_window(field, place, slot, term):
    base, low, col = spot(place, slot)
    for part in range(2):
        field[part, pl.ds(base, WIN + 8), :] += put_lanes(put_rows(term[part], low), col)


def assemble(place, field, layer, own, near, far, sibling, other, arrived):
    middle = [tile.at[layer] for tile in (own, near, far)]
    parts = pieces(place, field, middle, [sibling.at[k] for k in range(3)], [other.at[k] for k in range(3)])
    return [pltpu.make_async_copy(a, b, arrived.at[n]) for n, (a, b) in enumerate(parts)]


def front_kernel(place, own, near, far, sibling, other, probe, propagator, tables, out_wave, out_layer, field, arrived):
    loads = assemble(place, field, 0, own, near, far, sibling, other, arrived)
    for load in loads:
        load.start()
    wave = (probe[0].astype(F32), probe[1].astype(F32))
    spread = (propagator[0], propagator[1])
    for load in loads:
        load.wait()
    layers = [window(field, place, slot) for slot in range(2)]
    spectra = forward([times(wave, layer) for layer in layers], tables)
    entering = inverse([times(spectrum, spread) for spectrum in spectra], tables)
    for slot in range(2):
        for part in range(2):
            out_layer[slot, part] = layers[slot][part]
            out_wave[slot, part] = entering[slot][part]


def back_kernel(place, weight, own, near, far, sibling, other, waves, layers, probe, propagator, intensity, tables,
                out_own, out_near, out_far, out_sibling, out_other, out_last, out_probe, field, total0, total1, arrived, left_sem):
    loads = assemble(place, field, 1, own, near, far, sibling, other, arrived)
    for load in loads:
        load.start()
    totals = (total0, total1)

    def stores(layer):
        middle = [tile.at[layer] for tile in (out_own, out_near, out_far)]
        beside = [out_sibling.at[k, layer] for k in range(3)]
        beyond = [out_other.at[0, layer], out_other.at[1, layer], out_last.at[layer]]
        parts = pieces(place, totals[layer], middle, beside, beyond)
        return [pltpu.make_async_copy(b, a, left_sem.at[layer, n]) for n, (a, b) in enumerate(parts)]

    for total in totals:
        total[...] = jnp.zeros(total.shape, F32)
    spread = (propagator[0], propagator[1])
    for load in loads:
        load.wait()
    two = range(2)
    spectra = forward([times((waves[slot, 0], waves[slot, 1]), window(field, place, slot)) for slot in two], tables)
    fields = []
    for slot in two:
        spectrum = spectra[slot]
        power = spectrum[0] * spectrum[0] + spectrum[1] * spectrum[1]
        misfit = weight[slot] * (power - intensity[slot])
        fields.append((misfit * spectrum[0], misfit * spectrum[1]))
    adjoint = inverse(fields, tables)
    for slot in two:
        add_window(total1, place, slot, conj_times((waves[slot, 0], waves[slot, 1]), adjoint[slot]))
    upstream = [conj_times(window(field, place, slot), adjoint[slot]) for slot in two]
    for store in stores(1):
        store.start()
    wave = (probe[0].astype(F32), probe[1].astype(F32))
    spectra = forward(upstream, tables)
    adjoint = inverse([conj_times(spread, spectrum) for spectrum in spectra], tables)
    for slot in two:
        add_window(total0, place, slot, conj_times(wave, adjoint[slot]))
    for store in stores(0):
        store.start()
    upstream = [conj_times((layers[slot, 0], layers[slot, 1]), adjoint[slot]) for slot in two]
    blocks = out_probe.shape[0]
    for part in range(2):
        out_probe[:, part] = (upstream[0][part] + upstream[1][part]).reshape(blocks, WIN // blocks, WIN)
    for layer in range(2):
        for store in stores(layer):
            store.wait()


VMEM = pl.BlockSpec(memory_space=pltpu.VMEM)
SMEM = pl.BlockSpec(memory_space=pltpu.SMEM)
ANYWHERE = pl.BlockSpec(memory_space=pl.ANY)


def shaped(*shape):
    return jax.ShapeDtypeStruct(shape, F32)


def call(kernel, out_shape, in_specs, out_specs, scratch_shapes, flops):
    return pl.pallas_call(
        kernel,
        out_shape=out_shape,
        in_specs=in_specs,
        out_specs=out_specs,
        scratch_shapes=scratch_shapes,
        compiler_params=pltpu.CompilerParams(vmem_limit_bytes=24 * 1024 * 1024),
        cost_estimate=pl.CostEstimate(flops=flops, bytes_accessed=4_000_000, transcendentals=0),
    )


def hold_kernel(stored, out, arrived):
    load = pltpu.make_async_copy(stored, out, arrived)
    load.start()
    load.wait()


def hold(tables):
    return call(
        hold_kernel,
        jax.ShapeDtypeStruct(tables.shape, BF16),
        [ANYWHERE],
        VMEM,
        [pltpu.SemaphoreType.DMA],
        0,
    )(tables)


def front(place, tiles, probe, propagator, tables):
    return call(
        front_kernel,
        [shaped(2, 2, WIN, WIN)] * 2,
        [SMEM] + [ANYWHERE] * 5 + [VMEM] * 3,
        [VMEM] * 2,
        [pltpu.VMEM((2, 3 * HALF, 3 * HALF), F32), pltpu.SemaphoreType.DMA((9,))],
        3_300_000_000,
    )(place, *tiles, probe, propagator, tables)


def back(place, weight, tiles, waves, layers, probe, propagator, intensity, tables, blocks):
    return call(
        back_kernel,
        [shaped(2, 2, HALF, HALF)] * 3
        + [shaped(3, 2, 2, HALF, HALF), shaped(2, 2, 2, HALF, HALF), shaped(2, 2, HALF, HALF)]
        + [shaped(blocks, 2, WIN // blocks, WIN)],
        [SMEM] * 2 + [ANYWHERE] * 5 + [VMEM] * 6,
        [ANYWHERE] * 6 + [VMEM],
        [pltpu.VMEM((2, 3 * HALF, 3 * HALF), F32)] * 3
        + [pltpu.SemaphoreType.DMA((9,)), pltpu.SemaphoreType.DMA((2, 9))],
        6_600_000_000,
    )(place, weight, *tiles, waves, layers, probe, propagator, intensity, tables)


def flipped(pairs):
    return [(j, i) for i, j in pairs]


def sides(value):
    cols = lax.axis_size("col")
    inner = [(i, i + 1) for i in range(1, cols - 1, 2)]
    other = lax.ppermute(value, "col", inner + flipped(inner))
    return lax.ppermute(value, "col", [(i, i ^ 1) for i in range(cols)]), other


def probe_rows(term):
    rows = lax.axis_size("row")
    groups = [[2 * k + half for k in range(rows // 2)] for half in range(2)]
    return lax.all_to_all(term, "row", 0, 0, tiled=True, axis_index_groups=groups)


def probe_block(pair, own):
    rows, cols = (lax.axis_size("row"), lax.axis_size("col"))
    size, width = (WIN // rows, WIN // cols)
    parts = pair.reshape(2, 2, size, cols, width).transpose(1, 3, 0, 2, 4).reshape(2 * cols, 2, size * width)
    groups = [[(2 * k + half) * cols + c for half in range(2) for c in range(cols)] for k in range(rows // 2)]
    gathered = lax.all_to_all(parts, ("row", "col"), 0, 0, tiled=True, axis_index_groups=groups)
    own, gathered = lax.optimization_barrier((own, gathered))
    return own, jnp.sum(gathered, axis=0).reshape(2, size, width)


def per_device(object_slices, probe_wave, propagator_phase, intensity, centres, batch_order):
    rows = lax.axis_size("row")
    row, col = (lax.axis_index("row"), lax.axis_index("col"))
    hops = [(i, i + 2) for i in range(0, rows - 2, 2)] + [(i + 2, i) for i in range(1, rows - 2, 2)]
    swap = [(i, i ^ 1) for i in range(rows)]
    near = lax.ppermute(object_slices, "row", swap)
    order = order_matrix()
    angles = dot(dot(order, propagator_phase).astype(BF16), order.T)
    propagator = jnp.stack([jnp.cos(angles), jnp.sin(angles)])
    middle = jnp.einsum("ab,sbc->sac", order, intensity[0, 0], preferred_element_type=F32).astype(BF16)
    measured = jnp.einsum("sac,dc->sad", middle, order, preferred_element_type=F32)
    upper, odd = (row % 2, col % 2)
    place = jnp.concatenate([
        (centres[0, 0] - jnp.stack([row * HALF, col * HALF])).reshape(4),
        2 * HALF * jnp.stack([1 - upper, upper, 1 - odd, odd]),
    ]).astype(jnp.int32)
    weight = (batch_order[0, 0] >= 0).astype(F32)
    tables = hold(half_tables())
    ready = (near, propagator, measured, place, weight, tables)
    near, propagator, measured, place, weight, tables = lax.optimization_barrier(ready)
    far = lax.ppermute(near, "row", hops)
    tiles = (object_slices, near, far)
    stacks = lax.optimization_barrier([jnp.stack([object_slices[k], near[k], near[k]]) for k in range(2)])
    sent = [lax.dynamic_update_slice(stacks[k], far[k][None], (2, 0, 0, 0)) for k in range(2)]
    sides0, sides1 = (sides(sent[0]), sides(sent[1]))

    waves, layers = front(place, tiles + sides0, probe_wave, propagator, tables)
    outs = back(place, weight, tiles + sides1, waves, layers, probe_wave, propagator, measured, tables, rows // 2)
    own, near, far, to_sibling, to_other, to_last, probe_term = outs
    cols = lax.axis_size("col")
    inner = [(i, i + 1) for i in range(1, cols - 1, 2)]
    last = lax.ppermute(to_last, "col", inner + flipped(inner))
    other = lax.ppermute(to_other, "col", inner + flipped(inner))
    sibling = lax.ppermute(to_sibling, "col", [(i, i ^ 1) for i in range(cols)])
    spread = probe_rows(probe_term)
    far = lax.ppermute(far + sibling[2] + last, "row", flipped(hops))
    pair = jnp.sum(spread, axis=0)
    near = near + sibling[1] + other[1] + far
    own = own + sibling[0] + other[0] + lax.ppermute(near, "row", swap)
    return probe_block(pair, own)


def solution(mesh):
    placed = (
        P(None, None, "row", "col"),
        P(),
        P(),
        P("row", "col", None, None, None),
        P("row", "col", None, None),
        P("row", "col", None),
    )
    return jax.shard_map(
        per_device,
        mesh=mesh,
        in_specs=placed,
        out_specs=(P(None, None, "row", "col"), P(None, "row", "col")),
        check_vma=False,
    )
```
